32 devices in a mesh: groups: 2 (over y), samples: 4 (over z), blocks: 2 (over x), folds: 2 (over core).
Axes of the slice: x: 2, y: 2, z: 4, core: 2. Of those that a mesh axis runs over, the one named last changes fastest.
Arguments:
- allele_dosage_table: bfloat16 [1000, 4096], P('blocks', ('groups', 'samples')), parts along dimension 1, may hold values from -6 to 6
- phenotype_values: bfloat16 [20, 4096], P(None, ('groups', 'samples')), parts along dimension 1, may hold values from -8 to 8
- individual_partition_label: int32 [4096], P(('groups', 'samples')), parts along dimension 0, may hold values from 0 to 3, as said below
- shrink_strengths: float32 [2], replicated, may hold values from 0.005 to 2, as said below
Outputs:
- predictions: bfloat16 [4, 2, 2, 20, 1024], P('folds', 'blocks', None, None, ('groups', 'samples')), parts along dimension 4
- level_gram: float32 [8, 2, 2, 20, 2, 2], P(('groups', 'folds'), 'blocks'), parts along dimension 0
- level_cross: float32 [8, 2, 2, 20], P(('groups', 'folds'), 'blocks'), parts along dimension 0
The draws below stay inside these ranges and needn't reach their ends.
There are 2 independent parts, one for each index of `groups`. The reference program is written for one: setup_inputs(seed, part) draws one part's arguments, and reference() takes and returns one part's arrays. A program takes and returns all parts, laid end to end along the dimension named above; an argument that names none is the same for every part. Nothing has to cross between parts.
Inputs may be any that keep to these rules, and one draw needn't show every extreme that they name: `individual_partition_label`: among the 512 samples of each device (aligned runs of 512 indices) every fold number appears equally often, 512 / 4 times. `shrink_strengths`: the first penalty lies between 0.005 and 0.02, every other one between 0.1 and 2.
All inputs are finite; a program needn't handle non-finite values.
Results may differ from the reference program's by a relative error of at most 0.0055.
Values may be sent and summed in bfloat16 or wider, within the bound.
A program may use at most 64 MiB of HBM per device.

```python
import math
import jax
import jax.numpy as jnp
from jax import lax

BSIZE = 500
TRAITS = 20
SHRINK_LEVELS = 2
FOLDS = 4
SAMP_DEV = 512
SAMPLES = 2048
VARIANTS = 1000
N_BLOCKS = 2


def linked_chains(key):
    gap_key, second_gap_key, noise_key = jax.random.split(key, 3)
    first_low, first_high = (0.002, 0.2)
    second_low, second_high = (0.01, 0.5)
    first_weight = 0.8
    innovation = jax.random.normal(noise_key, (VARIANTS, 2, SAMPLES), jnp.float32)
    first_unit = jax.random.uniform(gap_key, (VARIANTS,), jnp.float32)
    second_unit = jax.random.uniform(second_gap_key, (VARIANTS,), jnp.float32)
    first_gap = jnp.exp(math.log(first_low) + first_unit * (math.log(first_high) - math.log(first_low)))
    second_gap = jnp.exp(math.log(second_low) + second_unit * (math.log(second_high) - math.log(second_low)))
    carry_rate = 1.0 - jnp.stack([first_gap, second_gap], axis=1)
    position = jnp.arange(VARIANTS, dtype=jnp.int32)[:, None]
    carry_rate = jnp.where(position == 0, 0.0, carry_rate).astype(jnp.float32)
    fresh_rate = jnp.sqrt(1.0 - carry_rate * carry_rate).astype(jnp.float32)

    def advance(state, inputs):
        rate, fresh, noise = inputs
        updated = rate[:, None] * state + fresh[:, None] * noise
        return (updated, updated)
    start = jnp.zeros((2, SAMPLES), jnp.float32)
    final_state, chains = lax.scan(advance, start, (carry_rate, fresh_rate, innovation))
    mixed = math.sqrt(first_weight) * chains[:, 0] + math.sqrt(1.0 - first_weight) * chains[:, 1]
    return jnp.clip(mixed, -6.0, 6.0)


def joint_draw(key):
    base = jax.random.fold_in(key, 17)
    chain_key, effect_key, trait_key = jax.random.split(base, 3)
    dosages = linked_chains(chain_key)
    effects = jax.random.normal(effect_key, (TRAITS, VARIANTS), jnp.float32) * math.sqrt(0.8 / VARIANTS)
    residual = math.sqrt(0.2) * jax.random.normal(trait_key, (TRAITS, SAMPLES), jnp.float32)
    values = jnp.dot(effects, dosages, precision=lax.Precision.HIGHEST) + residual
    return (dosages, jnp.clip(values, -8.0, 8.0))


def draw_allele_dosage_table(key, part):
    dosages, values = joint_draw(key)
    return dosages.astype(jnp.bfloat16)


def draw_phenotype_values(key, part):
    dosages, values = joint_draw(key)
    return values.astype(jnp.bfloat16)


def draw_individual_partition_label(key, part):
    shard_keys = jax.random.split(jax.random.fold_in(key, 29), SAMPLES // SAMP_DEV)
    pattern = jnp.arange(SAMP_DEV, dtype=jnp.int32) % FOLDS

    def shuffle(shard_key):
        return jax.random.permutation(shard_key, pattern)
    return jax.vmap(shuffle)(shard_keys).reshape(SAMPLES).astype(jnp.int32)


def draw_shrink_strengths(key, part):
    position = jnp.arange(SHRINK_LEVELS, dtype=jnp.int32)
    lower = jnp.where(position == 0, math.log(0.005), math.log(0.1)).astype(jnp.float32)
    upper = jnp.where(position == 0, math.log(0.02), math.log(2.0)).astype(jnp.float32)
    unit = jax.random.uniform(jax.random.fold_in(key, 41), (SHRINK_LEVELS,), jnp.float32)
    return jnp.exp(lower + unit * (upper - lower)).astype(jnp.float32)


def setup_inputs(seed: int = 0, part: int = 0) -> dict:
    arg_keys = jax.random.split(jax.random.key(seed), 5)
    part_splits = jax.random.split(jax.random.fold_in(arg_keys[4], part), 5)
    return {
        "allele_dosage_table": draw_allele_dosage_table(jax.random.fold_in(jax.random.fold_in(arg_keys[4], part), 71), part),
        "phenotype_values": draw_phenotype_values(jax.random.fold_in(jax.random.fold_in(arg_keys[4], part), 71), part),
        "individual_partition_label": draw_individual_partition_label(jax.random.fold_in(jax.random.fold_in(arg_keys[4], part), 71), part),
        "shrink_strengths": draw_shrink_strengths(jax.random.fold_in(arg_keys[4], 71), part),
    }


def segment_shrinkage_estimate(learning_design_inner, learning_design_response, shrink_strengths, individual_total):
    matrix_a = learning_design_inner / individual_total
    right_side = learning_design_response / individual_total
    identity = jnp.eye(learning_design_inner.shape[-1], dtype=jnp.float32)

    def lone_shrink_strength(value):
        factor = jnp.linalg.cholesky(matrix_a + value * identity)
        inner = lax.linalg.triangular_solve(factor, right_side, left_side=True, lower=True)
        return lax.linalg.triangular_solve(factor, inner, left_side=True, lower=True, transpose_a=True)
    return lax.map(lone_shrink_strength, shrink_strengths)

def reference(allele_dosage_table, phenotype_values, individual_partition_label, shrink_strengths):
    rows = SAMPLES // FOLDS
    learning_individual_tally = SAMPLES - rows
    sample_order = jnp.argsort(individual_partition_label, stable=True).astype(jnp.int32).reshape(FOLDS, rows)
    trait_sorted = jnp.take(phenotype_values, sample_order, axis=1).astype(jnp.float32)
    blocks_view = allele_dosage_table.reshape(N_BLOCKS, BSIZE, SAMPLES)

    def one_block(block):
        geno_sorted = jnp.take(block, sample_order, axis=1).astype(jnp.float32)
        held_gram = jnp.einsum('bki,cki->kbc', geno_sorted, geno_sorted, precision=lax.Precision.HIGHEST)
        held_cross = jnp.einsum('bki,pki->kbp', geno_sorted, trait_sorted, precision=lax.Precision.HIGHEST)
        learning_design_inner = jnp.sum(held_gram, 0)[None] - held_gram
        learning_design_response = jnp.sum(held_cross, 0)[None] - held_cross
        estimated_weights = segment_shrinkage_estimate(learning_design_inner, learning_design_response, shrink_strengths, learning_individual_tally)
        coefficient_half = lax.optimization_barrier(estimated_weights.astype(jnp.bfloat16)).astype(jnp.float32)
        preds = jnp.einsum('rkbp,bki->krpi', coefficient_half, geno_sorted, precision=lax.Precision.HIGHEST)
        return preds.astype(jnp.bfloat16)
    preds = lax.map(one_block, blocks_view)
    predictions = jnp.transpose(preds, (1, 0, 2, 3, 4))
    wide = lax.optimization_barrier(predictions).astype(jnp.float32)
    level_gram = jnp.einsum('kbrpi,kcspi->kbrpcs', wide, wide, precision=lax.Precision.HIGHEST) / rows
    level_cross = jnp.einsum('kbrpi,pki->kbrp', wide, trait_sorted, precision=lax.Precision.HIGHEST) / rows
    return (predictions, level_gram, level_cross)
```

```python
import functools

import jax
import jax.numpy as jnp
from jax import lax
from jax.experimental import pallas as pl
from jax.experimental.pallas import tpu as pltpu
from jax.sharding import PartitionSpec as P

SHRINK_LEVELS = 2
FOLDS = 4
PANEL = 128
MINI = 16


def dot_f32(a, b):
    return lax.dot_general(
        a, b, (((1,), (0,)), ((), ())), precision=lax.Precision.HIGHEST,
        preferred_element_type=jnp.float32,
    )


def sweep(block, m):
    low = m * MINI
    size = block.shape[0]
    rows = block[low:low + MINI, :]
    lane = lax.broadcasted_iota(jnp.int32, (MINI, size), 1)
    sub = lax.broadcasted_iota(jnp.int32, (MINI, size), 0)
    inside = (lane >= low) & (lane < low + MINI)
    cols = [jnp.broadcast_to(rows[:, low + j:low + j + 1], (MINI, size)) for j in range(MINI)]
    run = jnp.where(inside, jnp.where(lane - low == sub, 1.0, 0.0), rows)
    for j in range(MINI):
        inv = 1.0 / cols[j][j:j + 1, :]
        here = sub == j
        run_j = run[j:j + 1, :] * inv
        run = jnp.where(here, run_j, run - cols[j] * run_j)
        for i in range(j + 1, MINI):
            col_j = cols[i][j:j + 1, :] * inv
            cols[i] = jnp.where(here, col_j, cols[i] - cols[j] * col_j)
    lane = lax.broadcasted_iota(jnp.int32, (size, size), 1)
    sub = lax.broadcasted_iota(jnp.int32, (size, size), 0)
    in_cols = (lane >= low) & (lane < low + MINI)
    in_rows = (sub >= low) & (sub < low + MINI)
    left = jnp.where(in_cols & ~in_rows, block, 0.0)
    parts = []
    if low:
        parts.append(jnp.zeros((low, size), jnp.float32))
    parts.append(run)
    if low + MINI < size:
        parts.append(jnp.zeros((size - low - MINI, size), jnp.float32))
    placed = jnp.concatenate(parts, axis=0)
    kept = jnp.where(in_cols | in_rows, 0.0, block)
    rest = jnp.where(in_rows, placed, kept)
    return rest - dot_f32(left, placed)


def invert(work, strip):
    size = work.shape[0]

    def panel(p, carry):
        off = pl.multiple_of(p * PANEL, PANEL)
        here = pl.ds(off, PANEL)
        block = work[here, here]
        for m in range(PANEL // MINI):
            block = sweep(block, m)
        sub = lax.broadcasted_iota(jnp.int32, (size, PANEL), 0)
        col = jnp.where((sub >= off) & (sub < off + PANEL), 0.0, work[:, here])
        work[:, here] = jnp.zeros((size, PANEL), jnp.float32)
        strip[...] = dot_f32(block, work[here, :])
        strip[:, here] = block
        work[...] = work[...] - dot_f32(col, strip[...])
        work[here, :] = strip[...]
        return carry

    lax.fori_loop(0, size // PANEL, panel, 0)


def solve_kernel(tally, gram_ref, cross_ref, value_ref, out_ref, matrix, work, strip):
    size = work.shape[0]
    count = gram_ref.shape[0]
    value = value_ref[0]
    diagonal = lax.broadcasted_iota(jnp.int32, (size, size), 0) == lax.broadcasted_iota(
        jnp.int32, (size, size), 1
    )
    work[...] = jnp.where(diagonal, 1.0, 0.0)
    gram = gram_ref[...] / tally
    work[0:count, 0:count] = jnp.where(diagonal[0:count, 0:count], gram + value, gram)
    matrix[...] = work[...]
    right = jnp.concatenate(
        [cross_ref[...] / tally, jnp.zeros((size - count, cross_ref.shape[1]), jnp.float32)], axis=0
    )
    invert(work, strip)
    first = dot_f32(work[...], right)
    residual = right - dot_f32(matrix[...], first)
    second = first + dot_f32(work[...], residual)
    out_ref[...] = second[0:count, :].astype(out_ref.dtype)


def ridge_solve(gram, cross, value, tally):
    size = (gram.shape[0] + PANEL - 1) // PANEL * PANEL
    return pl.pallas_call(
        functools.partial(solve_kernel, tally),
        out_shape=jax.ShapeDtypeStruct(cross.shape, jnp.bfloat16),
        in_specs=[
            pl.BlockSpec(memory_space=pltpu.VMEM),
            pl.BlockSpec(memory_space=pltpu.VMEM),
            pl.BlockSpec(memory_space=pltpu.SMEM),
        ],
        out_specs=pl.BlockSpec(memory_space=pltpu.VMEM),
        scratch_shapes=[
            pltpu.VMEM((size, size), jnp.float32),
            pltpu.VMEM((size, size), jnp.float32),
            pltpu.VMEM((PANEL, size), jnp.float32),
        ],
        compiler_params=pltpu.CompilerParams(vmem_limit_bytes=32 * 1024 * 1024),
    )(gram, cross, value)


def per_device(allele_dosage_table, phenotype_values, individual_partition_label, shrink_strengths):
    own_count = FOLDS // lax.axis_size("folds")
    first = lax.axis_index("folds") * own_count
    rows_fold = allele_dosage_table.shape[1] // FOLDS
    total_rows = lax.axis_size("samples") * allele_dosage_table.shape[1]
    held_rows = total_rows // FOLDS
    learning_individual_tally = total_rows - held_rows
    sample_order = jnp.argsort(individual_partition_label, stable=True).reshape(FOLDS, rows_fold)
    geno_sorted = jnp.take(allele_dosage_table, sample_order, axis=1)
    trait_sorted = jnp.take(phenotype_values, sample_order, axis=1)
    geno_own = lax.dynamic_slice_in_dim(geno_sorted, first, own_count, 1)
    trait_own = lax.dynamic_slice_in_dim(trait_sorted, first, own_count, 1)
    held_gram = jnp.einsum(
        "bki,cki->kbc", geno_sorted, geno_sorted, preferred_element_type=jnp.float32
    )
    held_cross = jnp.einsum(
        "bki,pki->kbp", geno_sorted, trait_sorted, preferred_element_type=jnp.float32
    )
    own_gram = lax.dynamic_slice_in_dim(held_gram, first, own_count, 0)
    own_cross = lax.dynamic_slice_in_dim(held_cross, first, own_count, 0)
    learning_design_inner, learning_design_response = lax.psum(
        (jnp.sum(held_gram, 0)[None] - own_gram, jnp.sum(held_cross, 0)[None] - own_cross),
        "samples",
    )
    pair_total = own_count * SHRINK_LEVELS
    sample_devices = lax.axis_size("samples")
    per_processor = (pair_total + sample_devices - 1) // sample_devices
    pair_start = lax.axis_index("samples") * per_processor
    pair_ids = jnp.minimum(pair_start + jnp.arange(per_processor, dtype=jnp.int32), pair_total - 1)

    def one_pair(pair):
        fold_pick = pair // SHRINK_LEVELS
        ridge_pick = pair % SHRINK_LEVELS
        gram_one = lax.dynamic_index_in_dim(learning_design_inner, fold_pick, 0, keepdims=False)
        cross_one = lax.dynamic_index_in_dim(learning_design_response, fold_pick, 0, keepdims=False)
        value = lax.dynamic_slice_in_dim(shrink_strengths, ridge_pick, 1)
        return ridge_solve(gram_one, cross_one, value, float(learning_individual_tally))

    local_betas = jnp.stack([one_pair(pair_ids[i]) for i in range(per_processor)])
    gathered = lax.all_gather(local_betas, "samples", axis=0, tiled=True)[:pair_total]
    shaped = gathered.reshape(own_count, SHRINK_LEVELS, gathered.shape[1], gathered.shape[2])
    coefficient_half = jnp.transpose(shaped, (1, 0, 2, 3))
    preds = jnp.einsum(
        "rkbp,bki->krpi", coefficient_half, geno_own, preferred_element_type=jnp.float32
    ).astype(jnp.bfloat16)
    block_preds = preds[:, None]
    contrib = jnp.einsum(
        "krpi,kbspi->krpbs",
        preds,
        lax.all_gather(block_preds, "blocks", axis=1, tiled=True),
        preferred_element_type=jnp.float32,
    )
    cross_rows = jnp.einsum("krpi,pki->krp", preds, trait_own, preferred_element_type=jnp.float32)
    gram_sum, cross_sum = lax.psum((contrib, cross_rows), "samples")
    level_gram = gram_sum[:, None] / held_rows
    level_cross = cross_sum[:, None] / held_rows
    return (block_preds, level_gram, level_cross)


def solution(mesh):
    in_specs = (
        P("blocks", ("groups", "samples")),
        P(None, ("groups", "samples")),
        P(("groups", "samples")),
        P(),
    )
    out_specs = (
        P("folds", "blocks", None, None, ("groups", "samples")),
        P(("groups", "folds"), "blocks", None, None, None, None),
        P(("groups", "folds"), "blocks", None, None),
    )
    return jax.shard_map(
        per_device, mesh=mesh, in_specs=in_specs, out_specs=out_specs, check_vma=False
    )
```

```python
import functools

import jax
import jax.numpy as jnp
from jax import lax
from jax.experimental import pallas as pl
from jax.experimental.pallas import tpu as pltpu
from jax.sharding import PartitionSpec as P

SHRINK_LEVELS = 2
FOLDS = 4
PANEL = 128
MINI = 16


def dot_f32(a, b):
    return lax.dot_general(
        a, b, (((1,), (0,)), ((), ())), precision=lax.Precision.HIGHEST,
        preferred_element_type=jnp.float32,
    )


def sweep(block, m):
    low = m * MINI
    size = block.shape[0]
    rows = block[low:low + MINI, :]
    lane = lax.broadcasted_iota(jnp.int32, (MINI, size), 1)
    sub = lax.broadcasted_iota(jnp.int32, (MINI, size), 0)
    inside = (lane >= low) & (lane < low + MINI)
    cols = [jnp.broadcast_to(rows[:, low + j:low + j + 1], (MINI, size)) for j in range(MINI)]
    run = jnp.where(inside, jnp.where(lane - low == sub, 1.0, 0.0), rows)
    for j in range(MINI):
        inv = 1.0 / cols[j][j:j + 1, :]
        here = sub == j
        run_j = run[j:j + 1, :] * inv
        run = jnp.where(here, run_j, run - cols[j] * run_j)
        for i in range(j + 1, MINI):
            col_j = cols[i][j:j + 1, :] * inv
            cols[i] = jnp.where(here, col_j, cols[i] - cols[j] * col_j)
    lane = lax.broadcasted_iota(jnp.int32, (size, size), 1)
    sub = lax.broadcasted_iota(jnp.int32, (size, size), 0)
    in_cols = (lane >= low) & (lane < low + MINI)
    in_rows = (sub >= low) & (sub < low + MINI)
    left = jnp.where(in_cols & ~in_rows, block, 0.0)
    parts = []
    if low:
        parts.append(jnp.zeros((low, size), jnp.float32))
    parts.append(run)
    if low + MINI < size:
        parts.append(jnp.zeros((size - low - MINI, size), jnp.float32))
    placed = jnp.concatenate(parts, axis=0)
    kept = jnp.where(in_cols | in_rows, 0.0, block)
    rest = jnp.where(in_rows, placed, kept)
    return rest - dot_f32(left, placed)


def invert(work, strip):
    size = work.shape[0]

    def panel(p, carry):
        off = pl.multiple_of(p * PANEL, PANEL)
        here = pl.ds(off, PANEL)
        block = work[here, here]
        for m in range(PANEL // MINI):
            block = sweep(block, m)
        sub = lax.broadcasted_iota(jnp.int32, (size, PANEL), 0)
        col = jnp.where((sub >= off) & (sub < off + PANEL), 0.0, work[:, here])
        work[:, here] = jnp.zeros((size, PANEL), jnp.float32)
        strip[...] = dot_f32(block, work[here, :])
        strip[:, here] = block
        work[...] = work[...] - dot_f32(col, strip[...])
        work[here, :] = strip[...]
        return carry

    lax.fori_loop(0, size // PANEL, panel, 0)


def padded(count, multiple):
    return (count + multiple - 1) // multiple * multiple


def dot_nt(a, b):
    return lax.dot_general(a, b, (((1,), (1,)), ((), ())), preferred_element_type=jnp.float32)


def own_pair(total_pairs):
    place = lax.axis_index("samples") * lax.axis_size("folds") + lax.axis_index("folds")
    return lax.rem(place, total_pairs), place < total_pairs


def gather_kernel(shape, geno_ref, trait_ref, label_ref, gram_ref, held_ref, trait_own_ref,
                  stack, land, total, own_sem, next_sem, next_recv, side_sem, side_recv):
    chips, cores, variants, size, traits, part = shape
    z = lax.axis_index("samples")
    c = lax.axis_index("folds")
    width = stack.shape[1]
    rows_fold = width // FOLDS
    own_count = FOLDS // cores
    barrier = pltpu.get_barrier_semaphore()
    others = [lax.rem(c + o, cores) for o in range(1, cores)]
    has_left, has_right = z > 0, z < chips - 1

    def greet(axis, index):
        pl.semaphore_signal(barrier, inc=1, device_id={axis: index}, device_id_type=pl.DeviceIdType.MESH)

    for other in others:
        greet("folds", other)

    @pl.when(has_left)
    def _():
        greet("samples", z - 1)

    @pl.when(has_right)
    def _():
        greet("samples", z + 1)

    stack[...] = jnp.zeros_like(stack)
    stack[0:variants, :] = geno_ref[...]
    stack[size:size + traits, :] = trait_ref[...]
    label = label_ref[...]
    fold_row = lax.broadcasted_iota(jnp.int32, (16, width), 0)
    is_fold = fold_row == label
    earlier = lax.broadcasted_iota(jnp.int32, (width, width), 0) < lax.broadcasted_iota(
        jnp.int32, (width, width), 1
    )
    rank = jnp.dot(
        is_fold.astype(jnp.bfloat16), earlier.astype(jnp.bfloat16), preferred_element_type=jnp.float32
    )
    rank = jnp.sum(jnp.where(is_fold, rank, 0.0), axis=0, keepdims=True)
    target = rank + (label * rows_fold).astype(jnp.float32)
    places = lax.broadcasted_iota(jnp.int32, (width, width), 0).astype(jnp.float32)
    permute = (places == target).astype(jnp.bfloat16)
    ordered = dot_nt(stack[...], permute).astype(jnp.bfloat16)
    for q in range(FOLDS):
        for f in range(cores):
            land[z, q, f] = ordered[f * part:(f + 1) * part, q * rows_fold:(q + 1) * rows_fold]

    pl.semaphore_wait(barrier, len(others) + has_left.astype(jnp.int32) + has_right.astype(jnp.int32))

    def along(source, q, to, send):
        piece = land.at[source, q, c]
        return pltpu.make_async_remote_copy(
            src_ref=piece, dst_ref=piece, send_sem=send, recv_sem=next_recv.at[source, q],
            device_id={"samples": to}, device_id_type=pl.DeviceIdType.MESH,
        )

    def across(source, q, o):
        piece = land.at[source, q, c]
        return pltpu.make_async_remote_copy(
            src_ref=piece, dst_ref=piece, send_sem=side_sem.at[source, q, o],
            recv_sem=side_recv.at[source, q, o],
            device_id={"folds": others[o]}, device_id_type=pl.DeviceIdType.MESH,
        )

    for q in range(FOLDS):
        @pl.when(has_right)
        def _():
            along(z, q, z + 1, own_sem.at[0, q]).start()

        @pl.when(has_left)
        def _():
            along(z, q, z - 1, own_sem.at[1, q]).start()

    pair, _ = own_pair(FOLDS * SHRINK_LEVELS)
    fold = pair // SHRINK_LEVELS

    def add(source):
        columns = []
        for q in range(FOLDS):
            piece = jnp.concatenate([land[source, q, f] for f in range(cores)], axis=0)
            columns.append(jnp.where(fold == q, jnp.zeros_like(piece), piece))
        both = jnp.concatenate(columns, axis=1)
        total[...] += dot_nt(both, both[0:size, :])

    total[...] = jnp.zeros_like(total)
    add(z)

    def each_side(distance, fn):
        @pl.when(z - distance >= 0)
        def _():
            fn(z - distance, z + 1, has_right)

        @pl.when(z + distance < chips)
        def _():
            fn(z + distance, z - 1, has_left)

    def receive(distance, carry):
        for q in range(FOLDS):
            def relay(source, onward, more):
                along(source, q, z, next_sem.at[source, q]).wait_recv()

                @pl.when(more)
                def _():
                    along(source, q, onward, next_sem.at[source, q]).start()

                for o in range(cores - 1):
                    across(source, q, o).start()

            each_side(distance, relay)

        def collect(source, onward, more):
            for q in range(FOLDS):
                for o in range(cores - 1):
                    across(source, q, o).wait_recv()
            add(source)

        each_side(distance, collect)
        return carry

    lax.fori_loop(1, chips, receive, 0)
    gram_ref[...] = total[...]
    for s in range(chips):
        for f in range(cores):
            held_ref[s, f * part:(f + 1) * part, :] = land[s, fold, f]
        for k in range(own_count):
            last = jnp.concatenate([land[s, c * own_count + k, f] for f in range(cores)], axis=0)
            trait_own_ref[k, :, s * rows_fold:(s + 1) * rows_fold] = last[size:, :]

    for q in range(FOLDS):
        @pl.when(has_right)
        def _():
            along(z, q, z + 1, own_sem.at[0, q]).wait_send()

        @pl.when(has_left)
        def _():
            along(z, q, z - 1, own_sem.at[1, q]).wait_send()

    def finish(distance, carry):
        def sent(source, onward, more):
            for q in range(FOLDS):
                @pl.when(more)
                def _():
                    along(source, q, onward, next_sem.at[source, q]).wait_send()

                for o in range(cores - 1):
                    across(source, q, o).wait_send()

        each_side(distance, sent)
        return carry

    lax.fori_loop(1, chips, finish, 0)


def gather(geno, trait, label):
    chips, cores = lax.axis_size("samples"), lax.axis_size("folds")
    variants, width = geno.shape
    traits = trait.shape[0]
    size = padded(variants, PANEL)
    rows = padded(size + padded(traits, 16), 16 * cores)
    part = rows // cores
    rows_fold = width // FOLDS
    own_count = FOLDS // cores
    vmem = pl.BlockSpec(memory_space=pltpu.VMEM)
    return pl.pallas_call(
        functools.partial(gather_kernel, (chips, cores, variants, size, traits, part)),
        out_shape=(
            jax.ShapeDtypeStruct((rows, size), jnp.float32),
            jax.ShapeDtypeStruct((chips, rows, rows_fold), jnp.bfloat16),
            jax.ShapeDtypeStruct((own_count, rows - size, chips * rows_fold), jnp.bfloat16),
        ),
        in_specs=[vmem] * 3,
        out_specs=(vmem,) * 3,
        scratch_shapes=[
            pltpu.VMEM((rows, width), jnp.bfloat16),
            pltpu.VMEM((chips, FOLDS, cores, part, rows_fold), jnp.bfloat16),
            pltpu.VMEM((rows, size), jnp.float32),
            pltpu.SemaphoreType.DMA((2, FOLDS)),
            pltpu.SemaphoreType.DMA((chips, FOLDS)),
            pltpu.SemaphoreType.DMA((chips, FOLDS)),
            pltpu.SemaphoreType.DMA((chips, FOLDS, cores - 1)),
            pltpu.SemaphoreType.DMA((chips, FOLDS, cores - 1)),
        ],
        compiler_params=pltpu.CompilerParams(
            collective_id=0, has_side_effects=True, vmem_limit_bytes=48 * 1024 * 1024
        ),
    )(geno, trait, label.reshape(1, width))


def solve_kernel(variants, tally, gram_ref, held_ref, value_ref, out_ref, matrix, work, strip):
    size = work.shape[0]
    rows_fold = held_ref.shape[2]
    pair, _ = own_pair(FOLDS * SHRINK_LEVELS)
    value = value_ref[lax.rem(pair, SHRINK_LEVELS)]
    sub = lax.broadcasted_iota(jnp.int32, (size, size), 0)
    lane = lax.broadcasted_iota(jnp.int32, (size, size), 1)
    added = jnp.where(sub == lane, jnp.where(sub < variants, value, 1.0), 0.0)
    work[...] = gram_ref[0:size, :] / tally + added
    matrix[...] = work[...]
    right = gram_ref[size:, :] / tally
    invert(work, strip)
    first = dot_f32(right, work[...])
    residual = right - dot_f32(first, matrix[...])
    betas = (first + dot_f32(residual, work[...])).astype(jnp.bfloat16)
    for s in range(held_ref.shape[0]):
        preds = jnp.dot(betas, held_ref[s, 0:size, :], preferred_element_type=jnp.float32)
        out_ref[:, s * rows_fold:(s + 1) * rows_fold] = preds.astype(jnp.bfloat16)


def solve(gram, held, values, variants, tally):
    rows, size = gram.shape
    vmem = pl.BlockSpec(memory_space=pltpu.VMEM)
    return pl.pallas_call(
        functools.partial(solve_kernel, variants, tally),
        out_shape=jax.ShapeDtypeStruct((rows - size, held.shape[0] * held.shape[2]), jnp.bfloat16),
        in_specs=[vmem, vmem, pl.BlockSpec(memory_space=pltpu.SMEM)],
        out_specs=vmem,
        scratch_shapes=[
            pltpu.VMEM((size, size), jnp.float32),
            pltpu.VMEM((size, size), jnp.float32),
            pltpu.VMEM((PANEL, size), jnp.float32),
        ],
        compiler_params=pltpu.CompilerParams(vmem_limit_bytes=48 * 1024 * 1024),
    )(gram, held, values)


def exchange_kernel(shape, preds_ref, trait_ref, out_ref, gram_ref, cross_ref, slots, send_sem, recv_sem):
    chips, cores, blocks, traits = shape
    z = lax.axis_index("samples")
    c = lax.axis_index("folds")
    x = lax.axis_index("blocks")
    own_count = FOLDS // cores
    held = preds_ref.shape[1]
    rows_fold = held // chips
    pairs = FOLDS * SHRINK_LEVELS
    pair, reports = own_pair(pairs)
    fold, level = pair // SHRINK_LEVELS, lax.rem(pair, SHRINK_LEVELS)
    goal = fold // own_count
    local = lax.rem(fold, own_count)
    barrier = pltpu.get_barrier_semaphore()

    def is_self(dz, dx, dc):
        return (dz == z) & (dx == x) & (dc == c)

    senders = []
    for k in range(own_count):
        for r in range(SHRINK_LEVELS):
            place = (c * own_count + k) * SHRINK_LEVELS + r
            for b in range(blocks):
                senders.append((place // cores, b, lax.rem(place, cores), k, r))
    for sz, b, sc, k, r in senders:
        @pl.when(~is_self(sz, b, sc))
        def _():
            pl.semaphore_signal(
                barrier, inc=1, device_id={"samples": sz, "blocks": b, "folds": sc},
                device_id_type=pl.DeviceIdType.MESH,
            )

    targets = [(t, b) for t in range(chips) for b in range(blocks)]

    def message(n, t, b):
        return pltpu.make_async_remote_copy(
            src_ref=preds_ref, dst_ref=slots.at[local, x, level], send_sem=send_sem.at[n],
            recv_sem=recv_sem.at[local, x, level],
            device_id={"samples": t, "blocks": b, "folds": goal}, device_id_type=pl.DeviceIdType.MESH,
        )

    @pl.when(reports)
    def _():
        pl.semaphore_wait(barrier, len(targets) - (goal == c).astype(jnp.int32))
        for n, (t, b) in enumerate(targets):
            @pl.when(~is_self(t, b, goal))
            def _():
                message(n, t, b).start()

        @pl.when(goal == c)
        def _():
            slots[local, x, level] = preds_ref[...]

    for sz, b, sc, k, r in senders:
        @pl.when(~is_self(sz, b, sc))
        def _():
            piece = slots.at[k, b, r]
            pltpu.make_async_remote_copy(
                src_ref=piece, dst_ref=piece, send_sem=send_sem.at[0], recv_sem=recv_sem.at[k, b, r],
                device_id={"samples": sz}, device_id_type=pl.DeviceIdType.MESH,
            ).wait_recv()

    rows = slots.shape[3]
    lane = lax.broadcasted_iota(jnp.int32, (rows, gram_ref.shape[3]), 1)
    for k in range(own_count):
        trait = trait_ref[k].astype(jnp.float32)
        for r in range(SHRINK_LEVELS):
            mine = slots[k, x, r].astype(jnp.float32)
            out_ref[k, 0, r] = slots[k, x, r, 0:traits, pl.ds(pl.multiple_of(z * rows_fold, rows_fold), rows_fold)]
            block = jnp.zeros(lane.shape, jnp.float32)
            for b in range(blocks):
                for s in range(SHRINK_LEVELS):
                    theirs = slots[k, b, s].astype(jnp.float32)
                    one = jnp.sum(mine * theirs, axis=1, keepdims=True) / held
                    block = jnp.where(lane == b * SHRINK_LEVELS + s, one, block)
            gram_ref[k, r] = block
            one = jnp.sum(mine * trait, axis=1, keepdims=True) / held
            cross_ref[k, r] = jnp.where(lane == 0, one, 0.0)

    @pl.when(reports)
    def _():
        for n, (t, b) in enumerate(targets):
            @pl.when(~is_self(t, b, goal))
            def _():
                message(n, t, b).wait_send()


def exchange(preds, trait_own, traits):
    chips, cores, blocks = lax.axis_size("samples"), lax.axis_size("folds"), lax.axis_size("blocks")
    rows, held = preds.shape
    own_count = FOLDS // cores
    vmem = pl.BlockSpec(memory_space=pltpu.VMEM)
    lanes = padded(blocks * SHRINK_LEVELS, 128)
    return pl.pallas_call(
        functools.partial(exchange_kernel, (chips, cores, blocks, traits)),
        out_shape=(
            jax.ShapeDtypeStruct((own_count, 1, SHRINK_LEVELS, traits, held // chips), jnp.bfloat16),
            jax.ShapeDtypeStruct((own_count, SHRINK_LEVELS, rows, lanes), jnp.float32),
            jax.ShapeDtypeStruct((own_count, SHRINK_LEVELS, rows, lanes), jnp.float32),
        ),
        in_specs=[vmem] * 2,
        out_specs=(vmem,) * 3,
        scratch_shapes=[
            pltpu.VMEM((own_count, blocks, SHRINK_LEVELS, rows, held), jnp.bfloat16),
            pltpu.SemaphoreType.DMA((chips * blocks,)),
            pltpu.SemaphoreType.DMA((own_count, blocks, SHRINK_LEVELS)),
        ],
        compiler_params=pltpu.CompilerParams(
            collective_id=1, has_side_effects=True, vmem_limit_bytes=48 * 1024 * 1024
        ),
    )(preds, trait_own)


def per_device(allele_dosage_table, phenotype_values, individual_partition_label, shrink_strengths):
    blocks = lax.axis_size("blocks")
    variants, width = allele_dosage_table.shape
    traits = phenotype_values.shape[0]
    total_rows = lax.axis_size("samples") * width
    tally = float(total_rows - total_rows // FOLDS)
    gram, held, trait_own = gather(
        allele_dosage_table, phenotype_values, individual_partition_label
    )
    preds = solve(gram, held, shrink_strengths, variants, tally)
    predictions, level_gram, level_cross = exchange(preds, trait_own, traits)
    own_count = level_gram.shape[0]
    level_gram = level_gram[:, :, 0:traits, 0:blocks * SHRINK_LEVELS].reshape(
        own_count, 1, SHRINK_LEVELS, traits, blocks, SHRINK_LEVELS
    )
    level_cross = level_cross[:, None, :, 0:traits, 0]
    return (predictions, level_gram, level_cross)


def solution(mesh):
    in_specs = (
        P("blocks", ("groups", "samples")),
        P(None, ("groups", "samples")),
        P(("groups", "samples")),
        P(),
    )
    out_specs = (
        P("folds", "blocks", None, None, ("groups", "samples")),
        P(("groups", "folds"), "blocks", None, None, None, None),
        P(("groups", "folds"), "blocks", None, None),
    )
    return jax.shard_map(
        per_device, mesh=mesh, in_specs=in_specs, out_specs=out_specs, check_vma=False
    )
```

```python
import functools

import jax
import jax.numpy as jnp
from jax import lax
from jax.experimental import pallas as pl
from jax.experimental.pallas import tpu as pltpu
from jax.sharding import PartitionSpec as P

SHRINK_LEVELS = 2
FOLDS = 4
PANEL = 128
MINI = 16


def dot_f32(a, b):
    return lax.dot_general(
        a, b, (((1,), (0,)), ((), ())), precision=lax.Precision.HIGHEST,
        preferred_element_type=jnp.float32,
    )


def sweep(block, m):
    low = m * MINI
    size = block.shape[0]
    rows = block[low:low + MINI, :]
    lane = lax.broadcasted_iota(jnp.int32, (MINI, size), 1)
    sub = lax.broadcasted_iota(jnp.int32, (MINI, size), 0)
    inside = (lane >= low) & (lane < low + MINI)
    cols = [jnp.broadcast_to(rows[:, low + j:low + j + 1], (MINI, size)) for j in range(MINI)]
    run = jnp.where(inside, jnp.where(lane - low == sub, 1.0, 0.0), rows)
    for j in range(0, MINI, 2):
        a, c = cols[j][j:j + 1, :], cols[j][j + 1:j + 2, :]
        b, d = cols[j + 1][j:j + 1, :], cols[j + 1][j + 1:j + 2, :]
        scale = 1.0 / (a * d - b * c)
        is_first, is_second = sub == j, sub == j + 1
        pair = is_first | is_second
        left = jnp.where(pair, jnp.where(is_first, -1.0, 0.0), cols[j])
        right = jnp.where(pair, jnp.where(is_first, 0.0, -1.0), cols[j + 1])
        one = (right * c - left * d) * scale
        two = (left * b - right * a) * scale

        def eliminate(value):
            first, second = value[j:j + 1, :], value[j + 1:j + 2, :]
            return jnp.where(pair, 0.0, value) + (one * first + two * second)

        run = eliminate(run)
        for i in range(j + 2, MINI):
            cols[i] = eliminate(cols[i])
    lane = lax.broadcasted_iota(jnp.int32, (size, size), 1)
    sub = lax.broadcasted_iota(jnp.int32, (size, size), 0)
    in_cols = (lane >= low) & (lane < low + MINI)
    in_rows = (sub >= low) & (sub < low + MINI)
    left = jnp.where(in_cols & ~in_rows, block, 0.0)
    parts = []
    if low:
        parts.append(jnp.zeros((low, size), jnp.float32))
    parts.append(run)
    if low + MINI < size:
        parts.append(jnp.zeros((size - low - MINI, size), jnp.float32))
    placed = jnp.concatenate(parts, axis=0)
    kept = jnp.where(in_cols | in_rows, 0.0, block)
    rest = jnp.where(in_rows, placed, kept)
    return rest - dot_f32(left, placed)


def invert(work, strip):
    size = work.shape[0]

    def panel(p, carry):
        off = pl.multiple_of(p * PANEL, PANEL)
        here = pl.ds(off, PANEL)
        block = work[here, here]
        for m in range(PANEL // MINI):
            block = sweep(block, m)
        sub = lax.broadcasted_iota(jnp.int32, (size, PANEL), 0)
        col = jnp.where((sub >= off) & (sub < off + PANEL), 0.0, work[:, here])
        work[:, here] = jnp.zeros((size, PANEL), jnp.float32)
        strip[...] = dot_f32(block, work[here, :])
        strip[:, here] = block
        work[...] = work[...] - dot_f32(col, strip[...])
        work[here, :] = strip[...]
        return carry

    lax.fori_loop(0, size // PANEL, panel, 0)


def padded(count, multiple):
    return (count + multiple - 1) // multiple * multiple


def dot_nt(a, b):
    return lax.dot_general(a, b, (((1,), (1,)), ((), ())), preferred_element_type=jnp.float32)


def own_pair(total_pairs):
    place = lax.axis_index("samples") * lax.axis_size("folds") + lax.axis_index("folds")
    return lax.rem(place, total_pairs), place < total_pairs


def gather_kernel(shape, geno_ref, trait_ref, label_ref, gram_ref, held_ref, trait_own_ref,
                  stack, land, total, own_sem, next_sem, next_recv, side_sem, side_recv):
    chips, cores, variants, size, traits, part = shape
    z = lax.axis_index("samples")
    c = lax.axis_index("folds")
    width = stack.shape[1]
    rows_fold = width // FOLDS
    own_count = FOLDS // cores
    barrier = pltpu.get_barrier_semaphore()
    others = [lax.rem(c + o, cores) for o in range(1, cores)]
    has_left, has_right = z > 0, z < chips - 1

    def greet(axis, index):
        pl.semaphore_signal(barrier, inc=1, device_id={axis: index}, device_id_type=pl.DeviceIdType.MESH)

    for other in others:
        greet("folds", other)

    @pl.when(has_left)
    def _():
        greet("samples", z - 1)

    @pl.when(has_right)
    def _():
        greet("samples", z + 1)

    stack[...] = jnp.zeros_like(stack)
    stack[0:variants, :] = geno_ref[...]
    stack[size:size + traits, :] = trait_ref[...]
    label = label_ref[...]
    fold_row = lax.broadcasted_iota(jnp.int32, (16, width), 0)
    is_fold = fold_row == label
    earlier = lax.broadcasted_iota(jnp.int32, (width, width), 0) < lax.broadcasted_iota(
        jnp.int32, (width, width), 1
    )
    rank = jnp.dot(
        is_fold.astype(jnp.bfloat16), earlier.astype(jnp.bfloat16), preferred_element_type=jnp.float32
    )
    rank = jnp.sum(jnp.where(is_fold, rank, 0.0), axis=0, keepdims=True)
    target = rank + (label * rows_fold).astype(jnp.float32)
    places = lax.broadcasted_iota(jnp.int32, (width, width), 0).astype(jnp.float32)
    permute = (places == target).astype(jnp.bfloat16)
    ordered = dot_nt(stack[...], permute).astype(jnp.bfloat16)
    for q in range(FOLDS):
        for f in range(cores):
            land[z, q, f] = ordered[f * part:(f + 1) * part, q * rows_fold:(q + 1) * rows_fold]

    pl.semaphore_wait(barrier, len(others) + has_left.astype(jnp.int32) + has_right.astype(jnp.int32))

    def along(source, q, to, send):
        piece = land.at[source, q, c]
        return pltpu.make_async_remote_copy(
            src_ref=piece, dst_ref=piece, send_sem=send, recv_sem=next_recv.at[source, q],
            device_id={"samples": to}, device_id_type=pl.DeviceIdType.MESH,
        )

    def across(source, q, o):
        piece = land.at[source, q, c]
        return pltpu.make_async_remote_copy(
            src_ref=piece, dst_ref=piece, send_sem=side_sem.at[source, q, o],
            recv_sem=side_recv.at[source, q, o],
            device_id={"folds": others[o]}, device_id_type=pl.DeviceIdType.MESH,
        )

    for q in range(FOLDS):
        @pl.when(has_right)
        def _():
            along(z, q, z + 1, own_sem.at[0, q]).start()

        @pl.when(has_left)
        def _():
            along(z, q, z - 1, own_sem.at[1, q]).start()

    pair, _ = own_pair(FOLDS * SHRINK_LEVELS)
    fold = pair // SHRINK_LEVELS

    def add(source):
        columns = []
        for q in range(FOLDS):
            piece = jnp.concatenate([land[source, q, f] for f in range(cores)], axis=0)
            columns.append(jnp.where(fold == q, jnp.zeros_like(piece), piece))
        both = jnp.concatenate(columns, axis=1)
        total[...] += dot_nt(both, both[0:size, :])

    total[...] = jnp.zeros_like(total)
    add(z)

    def each_side(distance, fn):
        @pl.when(z - distance >= 0)
        def _():
            fn(z - distance, z + 1, has_right)

        @pl.when(z + distance < chips)
        def _():
            fn(z + distance, z - 1, has_left)

    def receive(distance, carry):
        for q in range(FOLDS):
            def relay(source, onward, more):
                along(source, q, z, next_sem.at[source, q]).wait_recv()

                @pl.when(more)
                def _():
                    along(source, q, onward, next_sem.at[source, q]).start()

                for o in range(cores - 1):
                    across(source, q, o).start()

            each_side(distance, relay)

        def collect(source, onward, more):
            for q in range(FOLDS):
                for o in range(cores - 1):
                    across(source, q, o).wait_recv()
            add(source)

        each_side(distance, collect)
        return carry

    lax.fori_loop(1, chips, receive, 0)
    gram_ref[...] = total[...]
    for s in range(chips):
        for f in range(cores):
            held_ref[s, f * part:(f + 1) * part, :] = land[s, fold, f]
        for k in range(own_count):
            last = jnp.concatenate([land[s, c * own_count + k, f] for f in range(cores)], axis=0)
            trait_own_ref[k, :, s * rows_fold:(s + 1) * rows_fold] = last[size:, :]

    for q in range(FOLDS):
        @pl.when(has_right)
        def _():
            along(z, q, z + 1, own_sem.at[0, q]).wait_send()

        @pl.when(has_left)
        def _():
            along(z, q, z - 1, own_sem.at[1, q]).wait_send()

    def finish(distance, carry):
        def sent(source, onward, more):
            for q in range(FOLDS):
                @pl.when(more)
                def _():
                    along(source, q, onward, next_sem.at[source, q]).wait_send()

                for o in range(cores - 1):
                    across(source, q, o).wait_send()

        each_side(distance, sent)
        return carry

    lax.fori_loop(1, chips, finish, 0)


def gather(geno, trait, label):
    chips, cores = lax.axis_size("samples"), lax.axis_size("folds")
    variants, width = geno.shape
    traits = trait.shape[0]
    size = padded(variants, PANEL)
    rows = padded(size + padded(traits, 16), 16 * cores)
    part = rows // cores
    rows_fold = width // FOLDS
    own_count = FOLDS // cores
    vmem = pl.BlockSpec(memory_space=pltpu.VMEM)
    return pl.pallas_call(
        functools.partial(gather_kernel, (chips, cores, variants, size, traits, part)),
        out_shape=(
            jax.ShapeDtypeStruct((rows, size), jnp.float32),
            jax.ShapeDtypeStruct((chips, rows, rows_fold), jnp.bfloat16),
            jax.ShapeDtypeStruct((own_count, rows - size, chips * rows_fold), jnp.bfloat16),
        ),
        in_specs=[vmem] * 3,
        out_specs=(vmem,) * 3,
        scratch_shapes=[
            pltpu.VMEM((rows, width), jnp.bfloat16),
            pltpu.VMEM((chips, FOLDS, cores, part, rows_fold), jnp.bfloat16),
            pltpu.VMEM((rows, size), jnp.float32),
            pltpu.SemaphoreType.DMA((2, FOLDS)),
            pltpu.SemaphoreType.DMA((chips, FOLDS)),
            pltpu.SemaphoreType.DMA((chips, FOLDS)),
            pltpu.SemaphoreType.DMA((chips, FOLDS, cores - 1)),
            pltpu.SemaphoreType.DMA((chips, FOLDS, cores - 1)),
        ],
        compiler_params=pltpu.CompilerParams(
            collective_id=0, has_side_effects=True, vmem_limit_bytes=48 * 1024 * 1024
        ),
    )(geno, trait, label.reshape(1, width))


def solve_kernel(variants, tally, gram_ref, held_ref, value_ref, out_ref, matrix, work, strip):
    size = work.shape[0]
    rows_fold = held_ref.shape[2]
    pair, _ = own_pair(FOLDS * SHRINK_LEVELS)
    value = value_ref[lax.rem(pair, SHRINK_LEVELS)]
    sub = lax.broadcasted_iota(jnp.int32, (size, size), 0)
    lane = lax.broadcasted_iota(jnp.int32, (size, size), 1)
    added = jnp.where(sub == lane, jnp.where(sub < variants, value, 1.0), 0.0)
    work[...] = gram_ref[0:size, :] / tally + added
    matrix[...] = work[...]
    right = gram_ref[size:, :] / tally
    invert(work, strip)
    first = dot_f32(right, work[...])
    residual = right - dot_f32(first, matrix[...])
    betas = (first + dot_f32(residual, work[...])).astype(jnp.bfloat16)
    for s in range(held_ref.shape[0]):
        preds = jnp.dot(betas, held_ref[s, 0:size, :], preferred_element_type=jnp.float32)
        out_ref[:, s * rows_fold:(s + 1) * rows_fold] = preds.astype(jnp.bfloat16)


def solve(gram, held, values, variants, tally):
    rows, size = gram.shape
    vmem = pl.BlockSpec(memory_space=pltpu.VMEM)
    return pl.pallas_call(
        functools.partial(solve_kernel, variants, tally),
        out_shape=jax.ShapeDtypeStruct((rows - size, held.shape[0] * held.shape[2]), jnp.bfloat16),
        in_specs=[vmem, vmem, pl.BlockSpec(memory_space=pltpu.SMEM)],
        out_specs=vmem,
        scratch_shapes=[
            pltpu.VMEM((size, size), jnp.float32),
            pltpu.VMEM((size, size), jnp.float32),
            pltpu.VMEM((PANEL, size), jnp.float32),
        ],
        compiler_params=pltpu.CompilerParams(vmem_limit_bytes=48 * 1024 * 1024),
    )(gram, held, values)


def exchange_kernel(shape, preds_ref, trait_ref, out_ref, gram_ref, cross_ref, slots, send_sem, recv_sem):
    chips, cores, blocks, traits = shape
    z = lax.axis_index("samples")
    c = lax.axis_index("folds")
    x = lax.axis_index("blocks")
    own_count = FOLDS // cores
    held = preds_ref.shape[1]
    rows_fold = held // chips
    pairs = FOLDS * SHRINK_LEVELS
    pair, reports = own_pair(pairs)
    fold, level = pair // SHRINK_LEVELS, lax.rem(pair, SHRINK_LEVELS)
    goal = fold // own_count
    local = lax.rem(fold, own_count)
    barrier = pltpu.get_barrier_semaphore()

    def is_self(dz, dx, dc):
        return (dz == z) & (dx == x) & (dc == c)

    senders = []
    for k in range(own_count):
        for r in range(SHRINK_LEVELS):
            place = (c * own_count + k) * SHRINK_LEVELS + r
            for b in range(blocks):
                senders.append((place // cores, b, lax.rem(place, cores), k, r))
    for sz, b, sc, k, r in senders:
        @pl.when(~is_self(sz, b, sc))
        def _():
            pl.semaphore_signal(
                barrier, inc=1, device_id={"samples": sz, "blocks": b, "folds": sc},
                device_id_type=pl.DeviceIdType.MESH,
            )

    targets = [(t, b) for t in range(chips) for b in range(blocks)]

    def message(n, t, b):
        return pltpu.make_async_remote_copy(
            src_ref=preds_ref, dst_ref=slots.at[local, x, level], send_sem=send_sem.at[n],
            recv_sem=recv_sem.at[local, x, level],
            device_id={"samples": t, "blocks": b, "folds": goal}, device_id_type=pl.DeviceIdType.MESH,
        )

    @pl.when(reports)
    def _():
        pl.semaphore_wait(barrier, len(targets) - (goal == c).astype(jnp.int32))
        for n, (t, b) in enumerate(targets):
            @pl.when(~is_self(t, b, goal))
            def _():
                message(n, t, b).start()

        @pl.when(goal == c)
        def _():
            slots[local, x, level] = preds_ref[...]

    for sz, b, sc, k, r in senders:
        @pl.when(~is_self(sz, b, sc))
        def _():
            piece = slots.at[k, b, r]
            pltpu.make_async_remote_copy(
                src_ref=piece, dst_ref=piece, send_sem=send_sem.at[0], recv_sem=recv_sem.at[k, b, r],
                device_id={"samples": sz}, device_id_type=pl.DeviceIdType.MESH,
            ).wait_recv()

    rows = slots.shape[3]
    lane = lax.broadcasted_iota(jnp.int32, (rows, gram_ref.shape[3]), 1)
    for k in range(own_count):
        trait = trait_ref[k].astype(jnp.float32)
        for r in range(SHRINK_LEVELS):
            mine = slots[k, x, r].astype(jnp.float32)
            out_ref[k, 0, r] = slots[k, x, r, 0:traits, pl.ds(pl.multiple_of(z * rows_fold, rows_fold), rows_fold)]
            block = jnp.zeros(lane.shape, jnp.float32)
            for b in range(blocks):
                for s in range(SHRINK_LEVELS):
                    theirs = slots[k, b, s].astype(jnp.float32)
                    one = jnp.sum(mine * theirs, axis=1, keepdims=True) / held
                    block = jnp.where(lane == b * SHRINK_LEVELS + s, one, block)
            gram_ref[k, r] = block
            one = jnp.sum(mine * trait, axis=1, keepdims=True) / held
            cross_ref[k, r] = jnp.where(lane == 0, one, 0.0)

    @pl.when(reports)
    def _():
        for n, (t, b) in enumerate(targets):
            @pl.when(~is_self(t, b, goal))
            def _():
                message(n, t, b).wait_send()


def exchange(preds, trait_own, traits):
    chips, cores, blocks = lax.axis_size("samples"), lax.axis_size("folds"), lax.axis_size("blocks")
    rows, held = preds.shape
    own_count = FOLDS // cores
    vmem = pl.BlockSpec(memory_space=pltpu.VMEM)
    lanes = padded(blocks * SHRINK_LEVELS, 128)
    return pl.pallas_call(
        functools.partial(exchange_kernel, (chips, cores, blocks, traits)),
        out_shape=(
            jax.ShapeDtypeStruct((own_count, 1, SHRINK_LEVELS, traits, held // chips), jnp.bfloat16),
            jax.ShapeDtypeStruct((own_count, SHRINK_LEVELS, rows, lanes), jnp.float32),
            jax.ShapeDtypeStruct((own_count, SHRINK_LEVELS, rows, lanes), jnp.float32),
        ),
        in_specs=[vmem] * 2,
        out_specs=(vmem,) * 3,
        scratch_shapes=[
            pltpu.VMEM((own_count, blocks, SHRINK_LEVELS, rows, held), jnp.bfloat16),
            pltpu.SemaphoreType.DMA((chips * blocks,)),
            pltpu.SemaphoreType.DMA((own_count, blocks, SHRINK_LEVELS)),
        ],
        compiler_params=pltpu.CompilerParams(
            collective_id=1, has_side_effects=True, vmem_limit_bytes=48 * 1024 * 1024
        ),
    )(preds, trait_own)


def per_device(allele_dosage_table, phenotype_values, individual_partition_label, shrink_strengths):
    blocks = lax.axis_size("blocks")
    variants, width = allele_dosage_table.shape
    traits = phenotype_values.shape[0]
    total_rows = lax.axis_size("samples") * width
    tally = float(total_rows - total_rows // FOLDS)
    gram, held, trait_own = gather(
        allele_dosage_table, phenotype_values, individual_partition_label
    )
    preds = solve(gram, held, shrink_strengths, variants, tally)
    predictions, level_gram, level_cross = exchange(preds, trait_own, traits)
    own_count = level_gram.shape[0]
    level_gram = level_gram[:, :, 0:traits, 0:blocks * SHRINK_LEVELS].reshape(
        own_count, 1, SHRINK_LEVELS, traits, blocks, SHRINK_LEVELS
    )
    level_cross = level_cross[:, None, :, 0:traits, 0]
    return (predictions, level_gram, level_cross)


def solution(mesh):
    in_specs = (
        P("blocks", ("groups", "samples")),
        P(None, ("groups", "samples")),
        P(("groups", "samples")),
        P(),
    )
    out_specs = (
        P("folds", "blocks", None, None, ("groups", "samples")),
        P(("groups", "folds"), "blocks", None, None, None, None),
        P(("groups", "folds"), "blocks", None, None),
    )
    return jax.shard_map(
        per_device, mesh=mesh, in_specs=in_specs, out_specs=out_specs, check_vma=False
    )
```

```python
import functools

import jax
import jax.numpy as jnp
from jax import lax
from jax.experimental import pallas as pl
from jax.experimental.pallas import tpu as pltpu
from jax.sharding import PartitionSpec as P

SHRINK_LEVELS = 2
FOLDS = 4
PANEL = 128
MINI = 16


def split(a):
    high = a.astype(jnp.bfloat16)
    rest = a - high.astype(jnp.float32)
    mid = rest.astype(jnp.bfloat16)
    low = (rest - mid.astype(jnp.float32)).astype(jnp.bfloat16)
    return high, mid, low


def dot_f32(a, b, a_dim=1):
    ah, am, al = split(a)
    bh, bm, bl = split(b)
    left = jnp.concatenate([ah, ah, am, am, ah, al], axis=a_dim)
    right = jnp.concatenate([bh, bm, bh, bm, bl, bh], axis=0)
    return lax.dot_general(
        left, right, (((a_dim,), (0,)), ((), ())), preferred_element_type=jnp.float32
    )


def sweep(block, m):
    low = m * MINI
    size = block.shape[0]
    rows = block[low:low + MINI, :]
    lane = lax.broadcasted_iota(jnp.int32, (MINI, size), 1)
    sub = lax.broadcasted_iota(jnp.int32, (MINI, size), 0)
    inside = (lane >= low) & (lane < low + MINI)
    cols = [jnp.broadcast_to(rows[:, low + j:low + j + 1], (MINI, size)) for j in range(MINI)]
    run = jnp.where(inside, jnp.where(lane - low == sub, 1.0, 0.0), rows)
    scale = jnp.zeros((MINI, size), jnp.float32)
    for j in range(MINI):
        inv = 1.0 / cols[j][j:j + 1, :]
        here = sub == j
        scale = jnp.where(here, inv, scale)
        ratio = jnp.where(here, 0.0, cols[j]) * inv
        run = run - ratio * run[j:j + 1, :]
        for i in range(j + 1, MINI):
            cols[i] = cols[i] - ratio * cols[i][j:j + 1, :]
    run = run * scale
    turned = jnp.where(inside, 0.0, jnp.where(lane < low, -rows, rows))
    update = dot_f32(turned, run, a_dim=0)

    def outside(start, stop):
        lane = lax.broadcasted_iota(jnp.int32, (stop - start, size), 1)
        kept = jnp.where((lane >= low) & (lane < low + MINI), 0.0, block[start:stop, :])
        return kept - update[start:stop, :]

    parts = []
    if low:
        parts.append(outside(0, low))
    parts.append(run)
    if low + MINI < size:
        parts.append(outside(low + MINI, size))
    return jnp.concatenate(parts, axis=0)


def invert(work, strip):
    size = work.shape[0]

    def panel(p, carry):
        off = pl.multiple_of(p * PANEL, PANEL)
        here = pl.ds(off, PANEL)
        block = work[here, here]
        for m in range(PANEL // MINI):
            block = sweep(block, m)
        sub = lax.broadcasted_iota(jnp.int32, (size, PANEL), 0)
        col = jnp.where((sub >= off) & (sub < off + PANEL), 0.0, work[:, here])
        work[:, here] = jnp.zeros((size, PANEL), jnp.float32)
        strip[...] = dot_f32(block, work[here, :])
        strip[:, here] = block
        work[...] = work[...] - dot_f32(col, strip[...])
        work[here, :] = strip[...]
        return carry

    lax.fori_loop(0, size // PANEL, panel, 0)


def padded(count, multiple):
    return (count + multiple - 1) // multiple * multiple


def dot_nt(a, b):
    return lax.dot_general(a, b, (((1,), (1,)), ((), ())), preferred_element_type=jnp.float32)


def own_pair(total_pairs):
    place = lax.axis_index("samples") * lax.axis_size("folds") + lax.axis_index("folds")
    return lax.rem(place, total_pairs), place < total_pairs


def gather_kernel(shape, geno_ref, trait_ref, label_ref, gram_ref, held_ref, trait_own_ref,
                  stack, land, total, own_sem, next_sem, next_recv, side_sem, side_recv):
    chips, cores, variants, size, traits, part = shape
    z = lax.axis_index("samples")
    c = lax.axis_index("folds")
    width = stack.shape[1]
    rows_fold = width // FOLDS
    own_count = FOLDS // cores
    barrier = pltpu.get_barrier_semaphore()
    others = [lax.rem(c + o, cores) for o in range(1, cores)]
    has_left, has_right = z > 0, z < chips - 1

    def greet(axis, index):
        pl.semaphore_signal(barrier, inc=1, device_id={axis: index}, device_id_type=pl.DeviceIdType.MESH)

    for other in others:
        greet("folds", other)

    @pl.when(has_left)
    def _():
        greet("samples", z - 1)

    @pl.when(has_right)
    def _():
        greet("samples", z + 1)

    stack[...] = jnp.zeros_like(stack)
    stack[0:variants, :] = geno_ref[...]
    stack[size:size + traits, :] = trait_ref[...]
    label = label_ref[...]
    fold_row = lax.broadcasted_iota(jnp.int32, (16, width), 0)
    is_fold = fold_row == label
    earlier = lax.broadcasted_iota(jnp.int32, (width, width), 0) < lax.broadcasted_iota(
        jnp.int32, (width, width), 1
    )
    rank = jnp.dot(
        is_fold.astype(jnp.bfloat16), earlier.astype(jnp.bfloat16), preferred_element_type=jnp.float32
    )
    rank = jnp.sum(jnp.where(is_fold, rank, 0.0), axis=0, keepdims=True)
    target = rank + (label * rows_fold).astype(jnp.float32)
    places = lax.broadcasted_iota(jnp.int32, (width, width), 0).astype(jnp.float32)
    permute = (places == target).astype(jnp.bfloat16)
    ordered = dot_nt(stack[...], permute).astype(jnp.bfloat16)
    for q in range(FOLDS):
        for f in range(cores):
            land[z, q, f] = ordered[f * part:(f + 1) * part, q * rows_fold:(q + 1) * rows_fold]

    pl.semaphore_wait(barrier, len(others) + has_left.astype(jnp.int32) + has_right.astype(jnp.int32))

    def along(source, q, to, send):
        piece = land.at[source, q, c]
        return pltpu.make_async_remote_copy(
            src_ref=piece, dst_ref=piece, send_sem=send, recv_sem=next_recv.at[source, q],
            device_id={"samples": to}, device_id_type=pl.DeviceIdType.MESH,
        )

    def across(source, q, o):
        piece = land.at[source, q, c]
        return pltpu.make_async_remote_copy(
            src_ref=piece, dst_ref=piece, send_sem=side_sem.at[source, q, o],
            recv_sem=side_recv.at[source, q, o],
            device_id={"folds": others[o]}, device_id_type=pl.DeviceIdType.MESH,
        )

    for q in range(FOLDS):
        @pl.when(has_right)
        def _():
            along(z, q, z + 1, own_sem.at[0, q]).start()

        @pl.when(has_left)
        def _():
            along(z, q, z - 1, own_sem.at[1, q]).start()

    pair, _ = own_pair(FOLDS * SHRINK_LEVELS)
    fold = pair // SHRINK_LEVELS

    def add(source):
        columns = []
        for q in range(FOLDS):
            piece = jnp.concatenate([land[source, q, f] for f in range(cores)], axis=0)
            columns.append(jnp.where(fold == q, jnp.zeros_like(piece), piece))
        both = jnp.concatenate(columns, axis=1)
        total[...] += dot_nt(both[0:size, :], both)

    total[...] = jnp.zeros_like(total)
    add(z)

    def each_side(distance, fn):
        @pl.when(z - distance >= 0)
        def _():
            fn(z - distance, z + 1, has_right)

        @pl.when(z + distance < chips)
        def _():
            fn(z + distance, z - 1, has_left)

    def receive(distance, carry):
        for q in range(FOLDS):
            def relay(source, onward, more):
                along(source, q, z, next_sem.at[source, q]).wait_recv()

                @pl.when(more)
                def _():
                    along(source, q, onward, next_sem.at[source, q]).start()

                for o in range(cores - 1):
                    across(source, q, o).start()

            each_side(distance, relay)

        def collect(source, onward, more):
            for q in range(FOLDS):
                for o in range(cores - 1):
                    across(source, q, o).wait_recv()
            add(source)

        each_side(distance, collect)
        return carry

    lax.fori_loop(1, chips, receive, 0)
    gram_ref[...] = total[...]
    for s in range(chips):
        for f in range(cores):
            held_ref[s, f * part:(f + 1) * part, :] = land[s, fold, f]
        for k in range(own_count):
            last = jnp.concatenate([land[s, c * own_count + k, f] for f in range(cores)], axis=0)
            trait_own_ref[k, :, s * rows_fold:(s + 1) * rows_fold] = last[size:, :]

    for q in range(FOLDS):
        @pl.when(has_right)
        def _():
            along(z, q, z + 1, own_sem.at[0, q]).wait_send()

        @pl.when(has_left)
        def _():
            along(z, q, z - 1, own_sem.at[1, q]).wait_send()

    def finish(distance, carry):
        def sent(source, onward, more):
            for q in range(FOLDS):
                @pl.when(more)
                def _():
                    along(source, q, onward, next_sem.at[source, q]).wait_send()

                for o in range(cores - 1):
                    across(source, q, o).wait_send()

        each_side(distance, sent)
        return carry

    lax.fori_loop(1, chips, finish, 0)


def gather(geno, trait, label):
    chips, cores = lax.axis_size("samples"), lax.axis_size("folds")
    variants, width = geno.shape
    traits = trait.shape[0]
    size = padded(variants, PANEL)
    rows = padded(size + padded(traits, 16), 16 * cores)
    part = rows // cores
    rows_fold = width // FOLDS
    own_count = FOLDS // cores
    vmem = pl.BlockSpec(memory_space=pltpu.VMEM)
    return pl.pallas_call(
        functools.partial(gather_kernel, (chips, cores, variants, size, traits, part)),
        out_shape=(
            jax.ShapeDtypeStruct((size, rows), jnp.float32),
            jax.ShapeDtypeStruct((chips, rows, rows_fold), jnp.bfloat16),
            jax.ShapeDtypeStruct((own_count, rows - size, chips * rows_fold), jnp.bfloat16),
        ),
        in_specs=[vmem] * 3,
        out_specs=(vmem,) * 3,
        scratch_shapes=[
            pltpu.VMEM((rows, width), jnp.bfloat16),
            pltpu.VMEM((chips, FOLDS, cores, part, rows_fold), jnp.bfloat16),
            pltpu.VMEM((size, rows), jnp.float32),
            pltpu.SemaphoreType.DMA((2, FOLDS)),
            pltpu.SemaphoreType.DMA((chips, FOLDS)),
            pltpu.SemaphoreType.DMA((chips, FOLDS)),
            pltpu.SemaphoreType.DMA((chips, FOLDS, cores - 1)),
            pltpu.SemaphoreType.DMA((chips, FOLDS, cores - 1)),
        ],
        compiler_params=pltpu.CompilerParams(
            collective_id=0, has_side_effects=True, vmem_limit_bytes=48 * 1024 * 1024
        ),
    )(geno, trait, label.reshape(1, width))


def solve_kernel(variants, tally, gram_ref, held_ref, value_ref, out_ref, matrix, work, strip):
    size = work.shape[0]
    rows_fold = held_ref.shape[2]
    pair, _ = own_pair(FOLDS * SHRINK_LEVELS)
    value = value_ref[lax.rem(pair, SHRINK_LEVELS)]
    sub = lax.broadcasted_iota(jnp.int32, (size, size), 0)
    lane = lax.broadcasted_iota(jnp.int32, (size, size), 1)
    added = jnp.where(sub == lane, jnp.where(sub < variants, value, 1.0), 0.0)
    work[...] = gram_ref[:, 0:size] / tally + added
    matrix[...] = work[...]
    right = gram_ref[:, size:] / tally
    invert(work, strip)
    first = dot_f32(work[...], right)
    residual = right - dot_f32(matrix[...], first)
    betas = (first + dot_f32(work[...], residual)).astype(jnp.bfloat16)
    for s in range(held_ref.shape[0]):
        preds = lax.dot_general(
            betas, held_ref[s, 0:size, :], (((0,), (0,)), ((), ())), preferred_element_type=jnp.float32
        )
        out_ref[:, s * rows_fold:(s + 1) * rows_fold] = preds.astype(jnp.bfloat16)


def solve(gram, held, values, variants, tally):
    size, rows = gram.shape
    vmem = pl.BlockSpec(memory_space=pltpu.VMEM)
    return pl.pallas_call(
        functools.partial(solve_kernel, variants, tally),
        out_shape=jax.ShapeDtypeStruct((rows - size, held.shape[0] * held.shape[2]), jnp.bfloat16),
        in_specs=[vmem, vmem, pl.BlockSpec(memory_space=pltpu.SMEM)],
        out_specs=vmem,
        scratch_shapes=[
            pltpu.VMEM((size, size), jnp.float32),
            pltpu.VMEM((size, size), jnp.float32),
            pltpu.VMEM((PANEL, size), jnp.float32),
        ],
        compiler_params=pltpu.CompilerParams(vmem_limit_bytes=48 * 1024 * 1024),
    )(gram, held, values)


def exchange_kernel(shape, preds_ref, trait_ref, out_ref, gram_ref, cross_ref, slots, send_sem, recv_sem):
    chips, cores, blocks, traits = shape
    z = lax.axis_index("samples")
    c = lax.axis_index("folds")
    x = lax.axis_index("blocks")
    own_count = FOLDS // cores
    held = preds_ref.shape[1]
    rows_fold = held // chips
    pairs = FOLDS * SHRINK_LEVELS
    pair, reports = own_pair(pairs)
    fold, level = pair // SHRINK_LEVELS, lax.rem(pair, SHRINK_LEVELS)
    goal = fold // own_count
    local = lax.rem(fold, own_count)
    barrier = pltpu.get_barrier_semaphore()

    def is_self(dz, dx, dc):
        return (dz == z) & (dx == x) & (dc == c)

    senders = []
    for k in range(own_count):
        for r in range(SHRINK_LEVELS):
            place = (c * own_count + k) * SHRINK_LEVELS + r
            for b in range(blocks):
                senders.append((place // cores, b, lax.rem(place, cores), k, r))
    for sz, b, sc, k, r in senders:
        @pl.when(~is_self(sz, b, sc))
        def _():
            pl.semaphore_signal(
                barrier, inc=1, device_id={"samples": sz, "blocks": b, "folds": sc},
                device_id_type=pl.DeviceIdType.MESH,
            )

    targets = [(t, b) for t in range(chips) for b in range(blocks)]

    def message(n, t, b):
        return pltpu.make_async_remote_copy(
            src_ref=preds_ref, dst_ref=slots.at[local, x, level], send_sem=send_sem.at[n],
            recv_sem=recv_sem.at[local, x, level],
            device_id={"samples": t, "blocks": b, "folds": goal}, device_id_type=pl.DeviceIdType.MESH,
        )

    @pl.when(reports)
    def _():
        pl.semaphore_wait(barrier, len(targets) - (goal == c).astype(jnp.int32))
        for n, (t, b) in enumerate(targets):
            @pl.when(~is_self(t, b, goal))
            def _():
                message(n, t, b).start()

        @pl.when(goal == c)
        def _():
            slots[local, x, level] = preds_ref[...]

    for sz, b, sc, k, r in senders:
        @pl.when(~is_self(sz, b, sc))
        def _():
            piece = slots.at[k, b, r]
            pltpu.make_async_remote_copy(
                src_ref=piece, dst_ref=piece, send_sem=send_sem.at[0], recv_sem=recv_sem.at[k, b, r],
                device_id={"samples": sz}, device_id_type=pl.DeviceIdType.MESH,
            ).wait_recv()

    rows = slots.shape[3]
    lane = lax.broadcasted_iota(jnp.int32, (rows, gram_ref.shape[3]), 1)
    for k in range(own_count):
        trait = trait_ref[k].astype(jnp.float32)
        for r in range(SHRINK_LEVELS):
            mine = slots[k, x, r].astype(jnp.float32)
            out_ref[k, 0, r] = slots[k, x, r, 0:traits, pl.ds(pl.multiple_of(z * rows_fold, rows_fold), rows_fold)]
            block = jnp.zeros(lane.shape, jnp.float32)
            for b in range(blocks):
                for s in range(SHRINK_LEVELS):
                    theirs = slots[k, b, s].astype(jnp.float32)
                    one = jnp.sum(mine * theirs, axis=1, keepdims=True) / held
                    block = jnp.where(lane == b * SHRINK_LEVELS + s, one, block)
            gram_ref[k, r] = block
            one = jnp.sum(mine * trait, axis=1, keepdims=True) / held
            cross_ref[k, r] = jnp.where(lane == 0, one, 0.0)

    @pl.when(reports)
    def _():
        for n, (t, b) in enumerate(targets):
            @pl.when(~is_self(t, b, goal))
            def _():
                message(n, t, b).wait_send()


def exchange(preds, trait_own, traits):
    chips, cores, blocks = lax.axis_size("samples"), lax.axis_size("folds"), lax.axis_size("blocks")
    rows, held = preds.shape
    own_count = FOLDS // cores
    vmem = pl.BlockSpec(memory_space=pltpu.VMEM)
    lanes = padded(blocks * SHRINK_LEVELS, 128)
    return pl.pallas_call(
        functools.partial(exchange_kernel, (chips, cores, blocks, traits)),
        out_shape=(
            jax.ShapeDtypeStruct((own_count, 1, SHRINK_LEVELS, traits, held // chips), jnp.bfloat16),
            jax.ShapeDtypeStruct((own_count, SHRINK_LEVELS, rows, lanes), jnp.float32),
            jax.ShapeDtypeStruct((own_count, SHRINK_LEVELS, rows, lanes), jnp.float32),
        ),
        in_specs=[vmem] * 2,
        out_specs=(vmem,) * 3,
        scratch_shapes=[
            pltpu.VMEM((own_count, blocks, SHRINK_LEVELS, rows, held), jnp.bfloat16),
            pltpu.SemaphoreType.DMA((chips * blocks,)),
            pltpu.SemaphoreType.DMA((own_count, blocks, SHRINK_LEVELS)),
        ],
        compiler_params=pltpu.CompilerParams(
            collective_id=1, has_side_effects=True, vmem_limit_bytes=48 * 1024 * 1024
        ),
    )(preds, trait_own)


def per_device(allele_dosage_table, phenotype_values, individual_partition_label, shrink_strengths):
    blocks = lax.axis_size("blocks")
    variants, width = allele_dosage_table.shape
    traits = phenotype_values.shape[0]
    total_rows = lax.axis_size("samples") * width
    tally = float(total_rows - total_rows // FOLDS)
    gram, held, trait_own = gather(
        allele_dosage_table, phenotype_values, individual_partition_label
    )
    preds = solve(gram, held, shrink_strengths, variants, tally)
    predictions, level_gram, level_cross = exchange(preds, trait_own, traits)
    own_count = level_gram.shape[0]
    level_gram = level_gram[:, :, 0:traits, 0:blocks * SHRINK_LEVELS].reshape(
        own_count, 1, SHRINK_LEVELS, traits, blocks, SHRINK_LEVELS
    )
    level_cross = level_cross[:, None, :, 0:traits, 0]
    return (predictions, level_gram, level_cross)


def solution(mesh):
    in_specs = (
        P("blocks", ("groups", "samples")),
        P(None, ("groups", "samples")),
        P(("groups", "samples")),
        P(),
    )
    out_specs = (
        P("folds", "blocks", None, None, ("groups", "samples")),
        P(("groups", "folds"), "blocks", None, None, None, None),
        P(("groups", "folds"), "blocks", None, None),
    )
    return jax.shard_map(
        per_device, mesh=mesh, in_specs=in_specs, out_specs=out_specs, check_vma=False
    )
```

```python
import functools

import jax
import jax.numpy as jnp
from jax import lax
from jax.experimental import pallas as pl
from jax.experimental.pallas import tpu as pltpu
from jax.sharding import PartitionSpec as P

SHRINK_LEVELS = 2
FOLDS = 4
PANEL = 128
MINI = 16


def split(a):
    high = a.astype(jnp.bfloat16)
    rest = a - high.astype(jnp.float32)
    mid = rest.astype(jnp.bfloat16)
    low = (rest - mid.astype(jnp.float32)).astype(jnp.bfloat16)
    return high, mid, low


def dot_f32(a, b, a_dim=1):
    ah, am, al = split(a)
    bh, bm, bl = split(b)
    left = jnp.concatenate([ah, ah, am, am, ah, al], axis=a_dim)
    right = jnp.concatenate([bh, bm, bh, bm, bl, bh], axis=0)
    return lax.dot_general(
        left, right, (((a_dim,), (0,)), ((), ())), preferred_element_type=jnp.float32
    )


def sweep(block, m):
    low = m * MINI
    size = block.shape[0]
    rows = block[low:low + MINI, :]
    lane = lax.broadcasted_iota(jnp.int32, (MINI, size), 1)
    sub = lax.broadcasted_iota(jnp.int32, (MINI, size), 0)
    inside = (lane >= low) & (lane < low + MINI)
    cols = [jnp.broadcast_to(rows[:, low + j:low + j + 1], (MINI, size)) for j in range(MINI)]
    run = jnp.where(inside, jnp.where(lane - low == sub, 1.0, 0.0), rows)
    scale = jnp.zeros((MINI, size), jnp.float32)
    for j in range(MINI):
        inv = 1.0 / cols[j][j:j + 1, :]
        here = sub == j
        scale = jnp.where(here, inv, scale)
        ratio = jnp.where(here, 0.0, cols[j]) * inv
        run = run - ratio * run[j:j + 1, :]
        for i in range(j + 1, MINI):
            cols[i] = cols[i] - ratio * cols[i][j:j + 1, :]
    run = run * scale
    turned = jnp.where(inside, 0.0, jnp.where(lane < low, -rows, rows))
    update = dot_f32(turned, run, a_dim=0)

    def outside(start, stop):
        lane = lax.broadcasted_iota(jnp.int32, (stop - start, size), 1)
        kept = jnp.where((lane >= low) & (lane < low + MINI), 0.0, block[start:stop, :])
        return kept - update[start:stop, :]

    parts = []
    if low:
        parts.append(outside(0, low))
    parts.append(run)
    if low + MINI < size:
        parts.append(outside(low + MINI, size))
    return jnp.concatenate(parts, axis=0)


def invert(work, strip, during):
    size = work.shape[0]

    def panel(p, carry):
        @pl.when(p == size // PANEL - 1)
        def _():
            during()

        off = pl.multiple_of(p * PANEL, PANEL)
        here = pl.ds(off, PANEL)
        block = work[here, here]
        for m in range(PANEL // MINI):
            block = sweep(block, m)
        sub = lax.broadcasted_iota(jnp.int32, (size, PANEL), 0)
        col = jnp.where((sub >= off) & (sub < off + PANEL), 0.0, work[:, here])
        work[:, here] = jnp.zeros((size, PANEL), jnp.float32)
        strip[...] = dot_f32(block, work[here, :])
        strip[:, here] = block
        work[...] = work[...] - dot_f32(col, strip[...])
        work[here, :] = strip[...]
        return carry

    lax.fori_loop(0, size // PANEL, panel, 0)


def padded(count, multiple):
    return (count + multiple - 1) // multiple * multiple


def dot_nt(a, b):
    return lax.dot_general(a, b, (((1,), (1,)), ((), ())), preferred_element_type=jnp.float32)


def own_pair(total_pairs):
    place = lax.axis_index("samples") * lax.axis_size("folds") + lax.axis_index("folds")
    return lax.rem(place, total_pairs), place < total_pairs


def kernel(shape, geno_hbm, trait_hbm, label_hbm, value_ref, out_ref, gram_ref, cross_ref,
           geno_ref, trait_ref, label_ref, stack, land, total, work, strip, preds_ref, slots,
           load_sem, own_sem, next_sem, next_recv, side_sem, side_recv, send_sem, recv_sem):
    chips, cores, blocks, variants, size, traits, part = shape
    z = lax.axis_index("samples")
    c = lax.axis_index("folds")
    x = lax.axis_index("blocks")
    width = stack.shape[1]
    rows_fold = width // FOLDS
    held = chips * rows_fold
    tally = chips * width - held
    own_count = FOLDS // cores
    pairs = FOLDS * SHRINK_LEVELS
    pair, reports = own_pair(pairs)
    fold, level = pair // SHRINK_LEVELS, lax.rem(pair, SHRINK_LEVELS)
    goal = fold // own_count
    local = lax.rem(fold, own_count)
    others = [lax.rem(c + o, cores) for o in range(1, cores)]
    has_left, has_right = z > 0, z < chips - 1
    last_right = ((chips - 1) * cores % pairs) // SHRINK_LEVELS
    last_left = 0
    early_right = [q for q in range(FOLDS) if q != last_right]
    early_left = [q for q in range(FOLDS) if q != last_left]

    loads = [
        pltpu.make_async_copy(source, goal_ref, load_sem.at[n])
        for n, (source, goal_ref) in enumerate(
            [(label_hbm, label_ref), (geno_hbm, geno_ref), (trait_hbm, trait_ref)]
        )
    ]
    for load in loads:
        load.start()

    barrier = pltpu.get_barrier_semaphore()

    def greet(**place):
        pl.semaphore_signal(barrier, inc=1, device_id=place, device_id_type=pl.DeviceIdType.MESH)

    for other in others:
        greet(folds=other)

    @pl.when(has_left)
    def _():
        greet(samples=z - 1)

    @pl.when(has_right)
    def _():
        greet(samples=z + 1)

    def is_self(dz, dx, dc):
        return (dz == z) & (dx == x) & (dc == c)

    senders = []
    for k in range(own_count):
        for r in range(SHRINK_LEVELS):
            place = (c * own_count + k) * SHRINK_LEVELS + r
            for b in range(blocks):
                senders.append((place // cores, b, lax.rem(place, cores), k, r))
    for sz, b, sc, k, r in senders:
        @pl.when(~is_self(sz, b, sc))
        def _():
            greet(samples=sz, blocks=b, folds=sc)

    targets = [(t, b) for t in range(chips) for b in range(blocks)]

    stack[...] = jnp.zeros_like(stack)
    total[...] = jnp.zeros_like(total)
    for load in loads:
        load.wait()
    stack[0:variants, :] = geno_ref[...]
    stack[size:size + traits, :] = trait_ref[...]
    label = label_ref[...]
    fold_row = lax.broadcasted_iota(jnp.int32, (16, width), 0)
    is_fold = fold_row == label
    earlier = lax.broadcasted_iota(jnp.int32, (width, width), 0) < lax.broadcasted_iota(
        jnp.int32, (width, width), 1
    )
    rank = jnp.dot(
        is_fold.astype(jnp.bfloat16), earlier.astype(jnp.bfloat16), preferred_element_type=jnp.float32
    )
    rank = jnp.sum(jnp.where(is_fold, rank, 0.0), axis=0, keepdims=True)
    target = rank + (label * rows_fold).astype(jnp.float32)
    places = lax.broadcasted_iota(jnp.int32, (width, width), 0).astype(jnp.float32)
    permute = (places == target).astype(jnp.bfloat16)
    ordered = dot_nt(stack[...], permute).astype(jnp.bfloat16)
    for q in range(FOLDS):
        for f in range(cores):
            land[z, q, f] = ordered[f * part:(f + 1) * part, q * rows_fold:(q + 1) * rows_fold]

    expected = len(others) + has_left.astype(jnp.int32) + has_right.astype(jnp.int32)
    farther = len(targets) - (goal == c).astype(jnp.int32)
    pl.semaphore_wait(barrier, expected + jnp.where(reports, farther, 0))

    def along(source, q, to, send):
        piece = land.at[source, q, c]
        return pltpu.make_async_remote_copy(
            src_ref=piece, dst_ref=piece, send_sem=send, recv_sem=next_recv.at[source, q],
            device_id={"samples": to}, device_id_type=pl.DeviceIdType.MESH,
        )

    def across(source, q, o):
        piece = land.at[source, q, c]
        return pltpu.make_async_remote_copy(
            src_ref=piece, dst_ref=piece, send_sem=side_sem.at[source, q, o],
            recv_sem=side_recv.at[source, q, o],
            device_id={"folds": others[o]}, device_id_type=pl.DeviceIdType.MESH,
        )

    def own_chunk(q, to_right):
        n, to = (0, z + 1) if to_right else (1, z - 1)
        return along(z, q, to, own_sem.at[n, q])

    for q_right, q_left in zip(early_right, early_left):
        @pl.when(has_right)
        def _():
            own_chunk(q_right, True).start()

        @pl.when(has_left)
        def _():
            own_chunk(q_left, False).start()

    def add(source, chunks):
        columns = []
        for q in chunks:
            piece = jnp.concatenate([land[source, q, f] for f in range(cores)], axis=0)
            columns.append(jnp.where(fold == q, jnp.zeros_like(piece), piece))
        both = jnp.concatenate(columns, axis=1)
        total[...] += dot_nt(both[0:size, :], both)

    add(z, range(FOLDS))

    def each_side(distance, fn):
        @pl.when(z - distance >= 0)
        def _():
            fn(z - distance, z + 1, has_right, early_right, last_right)

        @pl.when(z + distance < chips)
        def _():
            fn(z + distance, z - 1, has_left, early_left, last_left)

    def pass_on(source, q, onward, more):
        along(source, q, z, next_sem.at[source, q]).wait_recv()

        @pl.when(more)
        def _():
            along(source, q, onward, next_sem.at[source, q]).start()

        for o in range(cores - 1):
            across(source, q, o).start()

    def receive(distance, carry):
        for n in range(FOLDS - 1):
            each_side(distance, lambda source, onward, more, early, last: pass_on(source, early[n], onward, more))

        def collect(source, onward, more, early, last):
            for q in early:
                for o in range(cores - 1):
                    across(source, q, o).wait_recv()
            add(source, early)

        each_side(distance, collect)
        return carry

    lax.fori_loop(1, chips, receive, 0)

    @pl.when(has_right)
    def _():
        own_chunk(last_right, True).start()

    @pl.when(has_left)
    def _():
        own_chunk(last_left, False).start()

    def idle(more, last):
        return ~more & (fold == last)

    def receive_last(distance, carry):
        def relay(source, onward, more, early, last):
            @pl.when(~idle(more, last))
            def _():
                pass_on(source, last, onward, more)

        each_side(distance, relay)
        return carry

    def collect_last(distance, carry):
        def collect(source, onward, more, early, last):
            @pl.when(~idle(more, last))
            def _():
                for o in range(cores - 1):
                    across(source, last, o).wait_recv()
                add(source, [last])

        each_side(distance, collect)
        return carry

    lax.fori_loop(1, chips, receive_last, 0)
    lax.fori_loop(1, chips, collect_last, 0)

    def late():
        def step(distance, carry):
            def relay(source, onward, more, early, last):
                @pl.when(idle(more, last))
                def _():
                    pass_on(source, last, onward, more)

            each_side(distance, relay)
            return carry

        lax.fori_loop(1, chips, step, 0)

    sub = lax.broadcasted_iota(jnp.int32, (size, size), 0)
    lane = lax.broadcasted_iota(jnp.int32, (size, size), 1)
    value = jnp.where(level == 0, value_ref[0], value_ref[SHRINK_LEVELS - 1])
    for r in range(1, SHRINK_LEVELS - 1):
        value = jnp.where(level == r, value_ref[r], value)
    added = jnp.where(sub == lane, jnp.where(sub < variants, value, 1.0), 0.0)
    total[...] = total[...] * (1.0 / tally)
    total[:, 0:size] = total[:, 0:size] + added
    work[...] = total[:, 0:size]
    invert(work, strip, late)
    right = total[:, size:]
    first = dot_f32(work[...], right)
    residual = right - dot_f32(total[:, 0:size], first)
    betas = (first + dot_f32(work[...], residual)).astype(jnp.bfloat16)

    def late_done(distance, carry):
        def wait(source, onward, more, early, last):
            @pl.when(idle(more, last))
            def _():
                for o in range(cores - 1):
                    across(source, last, o).wait_recv()

        each_side(distance, wait)
        return carry

    lax.fori_loop(1, chips, late_done, 0)
    for s in range(chips):
        chunk = jnp.concatenate([land[s, fold, f] for f in range(cores)], axis=0)
        preds = lax.dot_general(
            betas, chunk[0:size, :], (((0,), (0,)), ((), ())), preferred_element_type=jnp.float32
        )
        preds_ref[:, s * rows_fold:(s + 1) * rows_fold] = preds.astype(jnp.bfloat16)

    def message(n, t, b):
        return pltpu.make_async_remote_copy(
            src_ref=preds_ref, dst_ref=slots.at[local, x, level], send_sem=send_sem.at[n],
            recv_sem=recv_sem.at[local, x, level],
            device_id={"samples": t, "blocks": b, "folds": goal}, device_id_type=pl.DeviceIdType.MESH,
        )

    @pl.when(reports)
    def _():
        for n, (t, b) in enumerate(targets):
            @pl.when(~is_self(t, b, goal))
            def _():
                message(n, t, b).start()

        @pl.when(goal == c)
        def _():
            slots[local, x, level] = preds_ref[...]

    for sz, b, sc, k, r in senders:
        @pl.when(~is_self(sz, b, sc))
        def _():
            piece = slots.at[k, b, r]
            pltpu.make_async_remote_copy(
                src_ref=piece, dst_ref=piece, send_sem=send_sem.at[0], recv_sem=recv_sem.at[k, b, r],
                device_id={"samples": sz}, device_id_type=pl.DeviceIdType.MESH,
            ).wait_recv()

    rows = slots.shape[3]
    lane = lax.broadcasted_iota(jnp.int32, (rows, gram_ref.shape[3]), 1)
    for k in range(own_count):
        pieces = []
        for s in range(chips):
            chunk = jnp.concatenate([land[s, c * own_count + k, f] for f in range(cores)], axis=0)
            pieces.append(chunk[size:, :])
        trait = jnp.concatenate(pieces, axis=1).astype(jnp.float32)
        for r in range(SHRINK_LEVELS):
            mine = slots[k, x, r].astype(jnp.float32)
            out_ref[k, 0, r] = slots[k, x, r, 0:traits, pl.ds(pl.multiple_of(z * rows_fold, rows_fold), rows_fold)]
            block = jnp.zeros(lane.shape, jnp.float32)
            for b in range(blocks):
                for s in range(SHRINK_LEVELS):
                    theirs = slots[k, b, s].astype(jnp.float32)
                    one = jnp.sum(mine * theirs, axis=1, keepdims=True) / held
                    block = jnp.where(lane == b * SHRINK_LEVELS + s, one, block)
            gram_ref[k, r] = block
            one = jnp.sum(mine * trait, axis=1, keepdims=True) / held
            cross_ref[k, r] = jnp.where(lane == 0, one, 0.0)

    @pl.when(reports)
    def _():
        for n, (t, b) in enumerate(targets):
            @pl.when(~is_self(t, b, goal))
            def _():
                message(n, t, b).wait_send()

    for q in range(FOLDS):
        @pl.when(has_right)
        def _():
            own_chunk(q, True).wait_send()

        @pl.when(has_left)
        def _():
            own_chunk(q, False).wait_send()

    def finish(distance, carry):
        def sent(source, onward, more, early, last):
            for q in range(FOLDS):
                @pl.when(more)
                def _():
                    along(source, q, onward, next_sem.at[source, q]).wait_send()

                for o in range(cores - 1):
                    across(source, q, o).wait_send()

        each_side(distance, sent)
        return carry

    lax.fori_loop(1, chips, finish, 0)


def per_device(allele_dosage_table, phenotype_values, individual_partition_label, shrink_strengths):
    chips, cores, blocks = lax.axis_size("samples"), lax.axis_size("folds"), lax.axis_size("blocks")
    variants, width = allele_dosage_table.shape
    traits = phenotype_values.shape[0]
    size = padded(variants, PANEL)
    rows = padded(size + padded(traits, 16), 16 * cores)
    part = rows // cores
    rows_fold = width // FOLDS
    held = chips * rows_fold
    own_count = FOLDS // cores
    lanes = padded(blocks * SHRINK_LEVELS, 128)
    vmem = pl.BlockSpec(memory_space=pltpu.VMEM)
    hbm = pl.BlockSpec(memory_space=pl.ANY)
    predictions, level_gram, level_cross = pl.pallas_call(
        functools.partial(kernel, (chips, cores, blocks, variants, size, traits, part)),
        out_shape=(
            jax.ShapeDtypeStruct((own_count, 1, SHRINK_LEVELS, traits, rows_fold), jnp.bfloat16),
            jax.ShapeDtypeStruct((own_count, SHRINK_LEVELS, rows - size, lanes), jnp.float32),
            jax.ShapeDtypeStruct((own_count, SHRINK_LEVELS, rows - size, lanes), jnp.float32),
        ),
        in_specs=[hbm, hbm, hbm, pl.BlockSpec(memory_space=pltpu.SMEM)],
        out_specs=(vmem,) * 3,
        scratch_shapes=[
            pltpu.VMEM((variants, width), jnp.bfloat16),
            pltpu.VMEM((traits, width), jnp.bfloat16),
            pltpu.VMEM((1, width), jnp.int32),
            pltpu.VMEM((rows, width), jnp.bfloat16),
            pltpu.VMEM((chips, FOLDS, cores, part, rows_fold), jnp.bfloat16),
            pltpu.VMEM((size, rows), jnp.float32),
            pltpu.VMEM((size, size), jnp.float32),
            pltpu.VMEM((PANEL, size), jnp.float32),
            pltpu.VMEM((rows - size, held), jnp.bfloat16),
            pltpu.VMEM((own_count, blocks, SHRINK_LEVELS, rows - size, held), jnp.bfloat16),
            pltpu.SemaphoreType.DMA((3,)),
            pltpu.SemaphoreType.DMA((2, FOLDS)),
            pltpu.SemaphoreType.DMA((chips, FOLDS)),
            pltpu.SemaphoreType.DMA((chips, FOLDS)),
            pltpu.SemaphoreType.DMA((chips, FOLDS, cores - 1)),
            pltpu.SemaphoreType.DMA((chips, FOLDS, cores - 1)),
            pltpu.SemaphoreType.DMA((chips * blocks,)),
            pltpu.SemaphoreType.DMA((own_count, blocks, SHRINK_LEVELS)),
        ],
        compiler_params=pltpu.CompilerParams(
            collective_id=0, has_side_effects=True, vmem_limit_bytes=60 * 1024 * 1024
        ),
    )(allele_dosage_table, phenotype_values, individual_partition_label.reshape(1, width), shrink_strengths)
    level_gram = level_gram[:, :, 0:traits, 0:blocks * SHRINK_LEVELS].reshape(
        own_count, 1, SHRINK_LEVELS, traits, blocks, SHRINK_LEVELS
    )
    level_cross = level_cross[:, None, :, 0:traits, 0]
    return (predictions, level_gram, level_cross)


def solution(mesh):
    in_specs = (
        P("blocks", ("groups", "samples")),
        P(None, ("groups", "samples")),
        P(("groups", "samples")),
        P(),
    )
    out_specs = (
        P("folds", "blocks", None, None, ("groups", "samples")),
        P(("groups", "folds"), "blocks", None, None, None, None),
        P(("groups", "folds"), "blocks", None, None),
    )
    return jax.shard_map(
        per_device, mesh=mesh, in_specs=in_specs, out_specs=out_specs, check_vma=False
    )
```

```python
import functools

import jax
import jax.numpy as jnp
from jax import lax
from jax.experimental import pallas as pl
from jax.experimental.pallas import tpu as pltpu
from jax.sharding import PartitionSpec as P

SHRINK_LEVELS = 2
FOLDS = 4
PANEL = 128
MINI = 16


def split(a):
    high = a.astype(jnp.bfloat16)
    rest = a - high.astype(jnp.float32)
    mid = rest.astype(jnp.bfloat16)
    low = (rest - mid.astype(jnp.float32)).astype(jnp.bfloat16)
    return high, mid, low


def dot_f32(a, b, a_dim=1):
    ah, am, al = split(a)
    bh, bm, bl = split(b)
    left = jnp.concatenate([ah, ah, am, am, ah, al], axis=a_dim)
    right = jnp.concatenate([bh, bm, bh, bm, bl, bh], axis=0)
    return lax.dot_general(
        left, right, (((a_dim,), (0,)), ((), ())), preferred_element_type=jnp.float32
    )


def sweep(block, m):
    low = m * MINI
    size = block.shape[0]
    rows = block[low:low + MINI, :]
    lane = lax.broadcasted_iota(jnp.int32, (MINI, size), 1)
    sub = lax.broadcasted_iota(jnp.int32, (MINI, size), 0)
    inside = (lane >= low) & (lane < low + MINI)
    cols = [jnp.broadcast_to(rows[:, low + j:low + j + 1], (MINI, size)) for j in range(MINI)]
    run = jnp.where(inside, jnp.where(lane - low == sub, 1.0, 0.0), rows)
    scale = jnp.zeros((MINI, size), jnp.float32)
    for j in range(MINI):
        inv = 1.0 / cols[j][j:j + 1, :]
        here = sub == j
        scale = jnp.where(here, inv, scale)
        ratio = jnp.where(here, 0.0, cols[j]) * inv
        run = run - ratio * run[j:j + 1, :]
        for i in range(j + 1, MINI):
            cols[i] = cols[i] - ratio * cols[i][j:j + 1, :]
    run = run * scale
    turned = jnp.where(inside, 0.0, jnp.where(lane < low, -rows, rows))
    update = dot_f32(turned, run, a_dim=0)

    def outside(start, stop):
        lane = lax.broadcasted_iota(jnp.int32, (stop - start, size), 1)
        kept = jnp.where((lane >= low) & (lane < low + MINI), 0.0, block[start:stop, :])
        return kept - update[start:stop, :]

    parts = []
    if low:
        parts.append(outside(0, low))
    parts.append(run)
    if low + MINI < size:
        parts.append(outside(low + MINI, size))
    return jnp.concatenate(parts, axis=0)


def invert(work, strip, during):
    size = work.shape[0]

    def panel(p, carry):
        @pl.when(p == size // PANEL - 1)
        def _():
            during()

        off = pl.multiple_of(p * PANEL, PANEL)
        here = pl.ds(off, PANEL)
        block = work[here, here]
        for m in range(PANEL // MINI):
            block = sweep(block, m)
        sub = lax.broadcasted_iota(jnp.int32, (size, PANEL), 0)
        col = jnp.where((sub >= off) & (sub < off + PANEL), 0.0, work[:, here])
        work[:, here] = jnp.zeros((size, PANEL), jnp.float32)
        strip[...] = dot_f32(block, work[here, :])
        strip[:, here] = block
        work[...] = work[...] - dot_f32(col, strip[...])
        work[here, :] = strip[...]
        return carry

    lax.fori_loop(0, size // PANEL, panel, 0)


def padded(count, multiple):
    return (count + multiple - 1) // multiple * multiple


def dot_nt(a, b):
    return lax.dot_general(a, b, (((1,), (1,)), ((), ())), preferred_element_type=jnp.float32)


def own_pair(total_pairs):
    place = lax.axis_index("samples") * lax.axis_size("folds") + lax.axis_index("folds")
    return lax.rem(place, total_pairs), place < total_pairs


def kernel(shape, geno_hbm, trait_hbm, label_hbm, value_ref, out_ref, gram_ref, cross_ref,
           geno_ref, trait_ref, label_ref, stack, land, total, work, strip, preds_ref, slots,
           load_sem, own_sem, next_sem, next_recv, side_sem, side_recv, send_sem, recv_sem):
    chips, cores, blocks, variants, size, traits, part = shape
    z = lax.axis_index("samples")
    c = lax.axis_index("folds")
    x = lax.axis_index("blocks")
    width = stack.shape[1]
    rows_fold = width // FOLDS
    held = chips * rows_fold
    tally = chips * width - held
    own_count = FOLDS // cores
    pairs = FOLDS * SHRINK_LEVELS
    pair, reports = own_pair(pairs)
    fold, level = pair // SHRINK_LEVELS, lax.rem(pair, SHRINK_LEVELS)
    goal = fold // own_count
    local = lax.rem(fold, own_count)
    others = [lax.rem(c + o, cores) for o in range(1, cores)]
    has_left, has_right = z > 0, z < chips - 1
    last_right = ((chips - 1) * cores % pairs) // SHRINK_LEVELS
    last_left = 0
    early_right = [q for q in range(FOLDS) if q != last_right]
    early_left = [q for q in range(FOLDS) if q != last_left]

    loads = [
        pltpu.make_async_copy(source, goal_ref, load_sem.at[n])
        for n, (source, goal_ref) in enumerate(
            [(label_hbm, label_ref), (geno_hbm, geno_ref), (trait_hbm, trait_ref)]
        )
    ]
    for load in loads:
        load.start()

    barrier = pltpu.get_barrier_semaphore()

    def greet(**place):
        pl.semaphore_signal(barrier, inc=1, device_id=place, device_id_type=pl.DeviceIdType.MESH)

    for other in others:
        greet(folds=other)

    @pl.when(has_left)
    def _():
        greet(samples=z - 1)

    @pl.when(has_right)
    def _():
        greet(samples=z + 1)

    def is_self(dz, dx, dc):
        return (dz == z) & (dx == x) & (dc == c)

    senders = []
    for k in range(own_count):
        for r in range(SHRINK_LEVELS):
            place = (c * own_count + k) * SHRINK_LEVELS + r
            for b in range(blocks):
                senders.append((place // cores, b, lax.rem(place, cores), k, r))
    for sz, b, sc, k, r in senders:
        @pl.when(~is_self(sz, b, sc))
        def _():
            greet(samples=sz, blocks=b, folds=sc)

    targets = [(t, b) for t in range(chips) for b in range(blocks)]

    stack[...] = jnp.zeros_like(stack)
    total[...] = jnp.zeros_like(total)
    for load in loads:
        load.wait()
    stack[0:variants, :] = geno_ref[...]
    stack[size:size + traits, :] = trait_ref[...]
    label = label_ref[...]
    fold_row = lax.broadcasted_iota(jnp.int32, (16, width), 0)
    is_fold = fold_row == label
    earlier = lax.broadcasted_iota(jnp.int32, (width, width), 0) < lax.broadcasted_iota(
        jnp.int32, (width, width), 1
    )
    rank = jnp.dot(
        is_fold.astype(jnp.bfloat16), earlier.astype(jnp.bfloat16), preferred_element_type=jnp.float32
    )
    rank = jnp.sum(jnp.where(is_fold, rank, 0.0), axis=0, keepdims=True)
    target = rank + (label * rows_fold).astype(jnp.float32)
    places = lax.broadcasted_iota(jnp.int32, (width, width), 0).astype(jnp.float32)
    permute = (places == target).astype(jnp.bfloat16)
    ordered = dot_nt(stack[...], permute).astype(jnp.bfloat16)
    for q in range(FOLDS):
        for f in range(cores):
            land[z, q, f] = ordered[f * part:(f + 1) * part, q * rows_fold:(q + 1) * rows_fold]

    expected = len(others) + has_left.astype(jnp.int32) + has_right.astype(jnp.int32)
    farther = len(targets) - (goal == c).astype(jnp.int32)
    pl.semaphore_wait(barrier, expected + jnp.where(reports, farther, 0))

    def along(source, q, to, send):
        piece = land.at[source, q, c]
        return pltpu.make_async_remote_copy(
            src_ref=piece, dst_ref=piece, send_sem=send, recv_sem=next_recv.at[source, q],
            device_id={"samples": to}, device_id_type=pl.DeviceIdType.MESH,
        )

    def across(source, q, o):
        piece = land.at[source, q, c]
        return pltpu.make_async_remote_copy(
            src_ref=piece, dst_ref=piece, send_sem=side_sem.at[source, q, o],
            recv_sem=side_recv.at[source, q, o],
            device_id={"folds": others[o]}, device_id_type=pl.DeviceIdType.MESH,
        )

    def own_chunk(q, to_right):
        n, to = (0, z + 1) if to_right else (1, z - 1)
        return along(z, q, to, own_sem.at[n, q])

    for q_right, q_left in zip(early_right, early_left):
        @pl.when(has_right)
        def _():
            own_chunk(q_right, True).start()

        @pl.when(has_left)
        def _():
            own_chunk(q_left, False).start()

    def add(source, chunks):
        columns = []
        for q in chunks:
            piece = jnp.concatenate([land[source, q, f] for f in range(cores)], axis=0)
            columns.append(jnp.where(fold == q, jnp.zeros_like(piece), piece))
        both = jnp.concatenate(columns, axis=1)
        total[...] += dot_nt(both[0:size, :], both)

    add(z, range(FOLDS))

    def each_side(distance, fn):
        @pl.when(z - distance >= 0)
        def _():
            fn(z - distance, z + 1, has_right, early_right, last_right)

        @pl.when(z + distance < chips)
        def _():
            fn(z + distance, z - 1, has_left, early_left, last_left)

    def pass_on(source, q, onward, more):
        along(source, q, z, next_sem.at[source, q]).wait_recv()

        @pl.when(more)
        def _():
            along(source, q, onward, next_sem.at[source, q]).start()

        for o in range(cores - 1):
            across(source, q, o).start()

    def collect(source, onward, more, early, last):
        for q in early:
            for o in range(cores - 1):
                across(source, q, o).wait_recv()
        add(source, early)

    def receive(distance, carry):
        for n in range(FOLDS - 1):
            each_side(distance, lambda source, onward, more, early, last: pass_on(source, early[n], onward, more))

        @pl.when((z == distance) & has_right)
        def _():
            own_chunk(last_right, True).start()

        @pl.when((z + distance == chips - 1) & has_left)
        def _():
            own_chunk(last_left, False).start()

        @pl.when(distance > 1)
        def _():
            each_side(distance - 1, collect)

        return carry

    @pl.when(~has_left & has_right)
    def _():
        own_chunk(last_right, True).start()

    @pl.when(~has_right & has_left)
    def _():
        own_chunk(last_left, False).start()

    lax.fori_loop(1, chips, receive, 0)

    def idle(more, last):
        return ~more & (fold == last)

    def receive_last(distance, carry):
        def relay(source, onward, more, early, last):
            @pl.when(~idle(more, last))
            def _():
                pass_on(source, last, onward, more)

        each_side(distance, relay)
        return carry

    def collect_last(distance, carry):
        def collect_one(source, onward, more, early, last):
            @pl.when(~idle(more, last))
            def _():
                for o in range(cores - 1):
                    across(source, last, o).wait_recv()
                add(source, [last])

        each_side(distance, collect_one)
        return carry

    lax.fori_loop(1, chips, receive_last, 0)
    if chips > 1:
        each_side(chips - 1, collect)
    lax.fori_loop(1, chips, collect_last, 0)

    def late():
        def step(distance, carry):
            def relay(source, onward, more, early, last):
                @pl.when(idle(more, last))
                def _():
                    pass_on(source, last, onward, more)

            each_side(distance, relay)
            return carry

        lax.fori_loop(1, chips, step, 0)

    sub = lax.broadcasted_iota(jnp.int32, (size, size), 0)
    lane = lax.broadcasted_iota(jnp.int32, (size, size), 1)
    value = jnp.where(level == 0, value_ref[0], value_ref[SHRINK_LEVELS - 1])
    for r in range(1, SHRINK_LEVELS - 1):
        value = jnp.where(level == r, value_ref[r], value)
    added = jnp.where(sub == lane, jnp.where(sub < variants, value, 1.0), 0.0)
    total[...] = total[...] * (1.0 / tally)
    total[:, 0:size] = total[:, 0:size] + added
    work[...] = total[:, 0:size]
    invert(work, strip, late)
    right = total[:, size:]
    first = dot_f32(work[...], right)
    residual = right - dot_f32(total[:, 0:size], first)
    betas = (first + dot_f32(work[...], residual)).astype(jnp.bfloat16)

    def late_done(distance, carry):
        def wait(source, onward, more, early, last):
            @pl.when(idle(more, last))
            def _():
                for o in range(cores - 1):
                    across(source, last, o).wait_recv()

        each_side(distance, wait)
        return carry

    lax.fori_loop(1, chips, late_done, 0)
    for s in range(chips):
        chunk = jnp.concatenate([land[s, fold, f] for f in range(cores)], axis=0)
        preds = lax.dot_general(
            betas, chunk[0:size, :], (((0,), (0,)), ((), ())), preferred_element_type=jnp.float32
        )
        preds_ref[:, s * rows_fold:(s + 1) * rows_fold] = preds.astype(jnp.bfloat16)

    def message(n, t, b):
        return pltpu.make_async_remote_copy(
            src_ref=preds_ref, dst_ref=slots.at[local, x, level], send_sem=send_sem.at[n],
            recv_sem=recv_sem.at[local, x, level],
            device_id={"samples": t, "blocks": b, "folds": goal}, device_id_type=pl.DeviceIdType.MESH,
        )

    @pl.when(reports)
    def _():
        for n, (t, b) in enumerate(targets):
            @pl.when(~is_self(t, b, goal))
            def _():
                message(n, t, b).start()

        @pl.when(goal == c)
        def _():
            slots[local, x, level] = preds_ref[...]

    for sz, b, sc, k, r in senders:
        @pl.when(~is_self(sz, b, sc))
        def _():
            piece = slots.at[k, b, r]
            pltpu.make_async_remote_copy(
                src_ref=piece, dst_ref=piece, send_sem=send_sem.at[0], recv_sem=recv_sem.at[k, b, r],
                device_id={"samples": sz}, device_id_type=pl.DeviceIdType.MESH,
            ).wait_recv()

    rows = slots.shape[3]

    def same_trait(mine, theirs):
        found = dot_nt(mine, theirs)
        at = lax.broadcasted_iota(jnp.int32, found.shape, 0)
        other = lax.rem(lax.broadcasted_iota(jnp.int32, found.shape, 1), rows)
        return jnp.sum(jnp.where(at == other, found, 0.0), axis=0, keepdims=True) / held

    for k in range(own_count):
        pieces = []
        for s in range(chips):
            chunk = jnp.concatenate([land[s, c * own_count + k, f] for f in range(cores)], axis=0)
            pieces.append(chunk[size:, :])
        trait = jnp.concatenate(pieces, axis=1)
        everything = jnp.concatenate(
            [slots[k, b, s] for b in range(blocks) for s in range(SHRINK_LEVELS)], axis=0
        )
        for r in range(SHRINK_LEVELS):
            mine = slots[k, x, r]
            out_ref[k, 0, r] = slots[k, x, r, 0:traits, pl.ds(pl.multiple_of(z * rows_fold, rows_fold), rows_fold)]
            gram_ref[k, r] = same_trait(mine, everything)
            cross_ref[k, r] = same_trait(mine, trait)

    @pl.when(reports)
    def _():
        for n, (t, b) in enumerate(targets):
            @pl.when(~is_self(t, b, goal))
            def _():
                message(n, t, b).wait_send()

    for q in range(FOLDS):
        @pl.when(has_right)
        def _():
            own_chunk(q, True).wait_send()

        @pl.when(has_left)
        def _():
            own_chunk(q, False).wait_send()

    def finish(distance, carry):
        def sent(source, onward, more, early, last):
            for q in range(FOLDS):
                @pl.when(more)
                def _():
                    along(source, q, onward, next_sem.at[source, q]).wait_send()

                for o in range(cores - 1):
                    across(source, q, o).wait_send()

        each_side(distance, sent)
        return carry

    lax.fori_loop(1, chips, finish, 0)


def per_device(allele_dosage_table, phenotype_values, individual_partition_label, shrink_strengths):
    chips, cores, blocks = lax.axis_size("samples"), lax.axis_size("folds"), lax.axis_size("blocks")
    variants, width = allele_dosage_table.shape
    traits = phenotype_values.shape[0]
    size = padded(variants, PANEL)
    rows = padded(size + padded(traits, 16), 16 * cores)
    part = rows // cores
    rows_fold = width // FOLDS
    held = chips * rows_fold
    own_count = FOLDS // cores
    vmem = pl.BlockSpec(memory_space=pltpu.VMEM)
    hbm = pl.BlockSpec(memory_space=pl.ANY)
    predictions, level_gram, level_cross = pl.pallas_call(
        functools.partial(kernel, (chips, cores, blocks, variants, size, traits, part)),
        out_shape=(
            jax.ShapeDtypeStruct((own_count, 1, SHRINK_LEVELS, traits, rows_fold), jnp.bfloat16),
            jax.ShapeDtypeStruct(
                (own_count, SHRINK_LEVELS, 1, blocks * SHRINK_LEVELS * (rows - size)), jnp.float32
            ),
            jax.ShapeDtypeStruct((own_count, SHRINK_LEVELS, 1, rows - size), jnp.float32),
        ),
        in_specs=[hbm, hbm, hbm, pl.BlockSpec(memory_space=pltpu.SMEM)],
        out_specs=(vmem,) * 3,
        scratch_shapes=[
            pltpu.VMEM((variants, width), jnp.bfloat16),
            pltpu.VMEM((traits, width), jnp.bfloat16),
            pltpu.VMEM((1, width), jnp.int32),
            pltpu.VMEM((rows, width), jnp.bfloat16),
            pltpu.VMEM((chips, FOLDS, cores, part, rows_fold), jnp.bfloat16),
            pltpu.VMEM((size, rows), jnp.float32),
            pltpu.VMEM((size, size), jnp.float32),
            pltpu.VMEM((PANEL, size), jnp.float32),
            pltpu.VMEM((rows - size, held), jnp.bfloat16),
            pltpu.VMEM((own_count, blocks, SHRINK_LEVELS, rows - size, held), jnp.bfloat16),
            pltpu.SemaphoreType.DMA((3,)),
            pltpu.SemaphoreType.DMA((2, FOLDS)),
            pltpu.SemaphoreType.DMA((chips, FOLDS)),
            pltpu.SemaphoreType.DMA((chips, FOLDS)),
            pltpu.SemaphoreType.DMA((chips, FOLDS, cores - 1)),
            pltpu.SemaphoreType.DMA((chips, FOLDS, cores - 1)),
            pltpu.SemaphoreType.DMA((chips * blocks,)),
            pltpu.SemaphoreType.DMA((own_count, blocks, SHRINK_LEVELS)),
        ],
        compiler_params=pltpu.CompilerParams(
            collective_id=0, has_side_effects=True, vmem_limit_bytes=60 * 1024 * 1024
        ),
    )(allele_dosage_table, phenotype_values, individual_partition_label.reshape(1, width), shrink_strengths)
    level_gram = level_gram.reshape(
        own_count, 1, SHRINK_LEVELS, blocks, SHRINK_LEVELS, rows - size
    )[..., 0:traits]
    level_gram = jnp.transpose(level_gram, (0, 1, 2, 5, 3, 4))
    level_cross = jnp.transpose(level_cross, (0, 2, 1, 3))[..., 0:traits]
    return (predictions, level_gram, level_cross)


def solution(mesh):
    in_specs = (
        P("blocks", ("groups", "samples")),
        P(None, ("groups", "samples")),
        P(("groups", "samples")),
        P(),
    )
    out_specs = (
        P("folds", "blocks", None, None, ("groups", "samples")),
        P(("groups", "folds"), "blocks", None, None, None, None),
        P(("groups", "folds"), "blocks", None, None),
    )
    return jax.shard_map(
        per_device, mesh=mesh, in_specs=in_specs, out_specs=out_specs, check_vma=False
    )
```

```python
import functools

import jax
import jax.numpy as jnp
from jax import lax
from jax.experimental import pallas as pl
from jax.experimental.pallas import tpu as pltpu
from jax.sharding import PartitionSpec as P

SHRINK_LEVELS = 2
FOLDS = 4
PANEL = 128
MINI = 16


def split(a):
    high = a.astype(jnp.bfloat16)
    rest = a - high.astype(jnp.float32)
    mid = rest.astype(jnp.bfloat16)
    low = (rest - mid.astype(jnp.float32)).astype(jnp.bfloat16)
    return high, mid, low


def dot_f32(a, b, a_dim=1):
    ah, am, al = split(a)
    bh, bm, bl = split(b)
    left = jnp.concatenate([ah, ah, am, am, ah, al], axis=a_dim)
    right = jnp.concatenate([bh, bm, bh, bm, bl, bh], axis=0)
    return lax.dot_general(
        left, right, (((a_dim,), (0,)), ((), ())), preferred_element_type=jnp.float32
    )


def rows_times(a, parts):
    count = a.shape[0]
    stacked = jnp.concatenate(split(a), axis=0)
    total = None
    for n, part in enumerate(parts):
        found = jnp.dot(stacked[0:(3 - n) * count, :], part, preferred_element_type=jnp.float32)
        for i in range(3 - n):
            one = found[i * count:(i + 1) * count, :]
            total = one if total is None else total + one
    return total


def sweep(block, m):
    low = m * MINI
    size = block.shape[0]
    rows = block[low:low + MINI, :]
    lane = lax.broadcasted_iota(jnp.int32, (MINI, size), 1)
    sub = lax.broadcasted_iota(jnp.int32, (MINI, size), 0)
    inside = (lane >= low) & (lane < low + MINI)
    cols = [jnp.broadcast_to(rows[:, low + j:low + j + 1], (MINI, size)) for j in range(MINI)]
    run = jnp.where(inside, jnp.where(lane - low == sub, 1.0, 0.0), rows)
    scale = jnp.zeros((MINI, size), jnp.float32)
    for j in range(MINI):
        inv = 1.0 / cols[j][j:j + 1, :]
        here = sub == j
        scale = jnp.where(here, inv, scale)
        ratio = jnp.where(here, 0.0, cols[j]) * inv
        run = run - ratio * run[j:j + 1, :]
        for i in range(j + 1, MINI):
            cols[i] = cols[i] - ratio * cols[i][j:j + 1, :]
    run = run * scale
    turned = jnp.where(inside, 0.0, jnp.where(lane < low, -rows, rows))
    update = dot_f32(turned, run, a_dim=0)

    def outside(start, stop):
        lane = lax.broadcasted_iota(jnp.int32, (stop - start, size), 1)
        kept = jnp.where((lane >= low) & (lane < low + MINI), 0.0, block[start:stop, :])
        return kept - update[start:stop, :]

    parts = []
    if low:
        parts.append(outside(0, low))
    parts.append(run)
    if low + MINI < size:
        parts.append(outside(low + MINI, size))
    return jnp.concatenate(parts, axis=0)


def invert(work, strip, during):
    size = work.shape[0]

    def panel(p, carry):
        @pl.when(p == size // PANEL - 1)
        def _():
            during()

        off = pl.multiple_of(p * PANEL, PANEL)
        here = pl.ds(off, PANEL)
        block = work[here, here]
        for m in range(PANEL // MINI):
            block = sweep(block, m)
        sub = lax.broadcasted_iota(jnp.int32, (size, PANEL), 0)
        col = jnp.where((sub >= off) & (sub < off + PANEL), 0.0, work[:, here])
        work[:, here] = jnp.zeros((size, PANEL), jnp.float32)
        strip[...] = dot_f32(block, work[here, :])
        strip[:, here] = block
        work[...] = work[...] - dot_f32(col, strip[...])
        work[here, :] = strip[...]
        return carry

    lax.fori_loop(0, size // PANEL, panel, 0)


def padded(count, multiple):
    return (count + multiple - 1) // multiple * multiple


def dot_nt(a, b):
    return lax.dot_general(a, b, (((1,), (1,)), ((), ())), preferred_element_type=jnp.float32)


def own_pair(total_pairs):
    place = lax.axis_index("samples") * lax.axis_size("folds") + lax.axis_index("folds")
    return lax.rem(place, total_pairs), place < total_pairs


def kernel(shape, geno_hbm, trait_hbm, label_hbm, value_ref, out_ref, gram_ref, cross_ref,
           geno_ref, trait_ref, label_ref, stack, land, total, work, strip, preds_ref, slots,
           load_sem, own_sem, next_sem, next_recv, side_sem, side_recv, send_sem, recv_sem):
    chips, cores, blocks, variants, size, traits, part = shape
    z = lax.axis_index("samples")
    c = lax.axis_index("folds")
    x = lax.axis_index("blocks")
    width = stack.shape[1]
    rows_fold = width // FOLDS
    held = chips * rows_fold
    tally = chips * width - held
    own_count = FOLDS // cores
    pairs = FOLDS * SHRINK_LEVELS
    pair, reports = own_pair(pairs)
    fold, level = pair // SHRINK_LEVELS, lax.rem(pair, SHRINK_LEVELS)
    goal = fold // own_count
    local = lax.rem(fold, own_count)
    others = [lax.rem(c + o, cores) for o in range(1, cores)]
    has_left, has_right = z > 0, z < chips - 1
    last_right = ((chips - 1) * cores % pairs) // SHRINK_LEVELS
    last_left = 0
    early_right = [q for q in range(FOLDS) if q != last_right]
    early_left = [q for q in range(FOLDS) if q != last_left]

    loads = [
        pltpu.make_async_copy(source, goal_ref, load_sem.at[n])
        for n, (source, goal_ref) in enumerate(
            [(label_hbm, label_ref), (geno_hbm, geno_ref), (trait_hbm, trait_ref)]
        )
    ]
    for load in loads:
        load.start()

    barrier = pltpu.get_barrier_semaphore()

    def greet(**place):
        pl.semaphore_signal(barrier, inc=1, device_id=place, device_id_type=pl.DeviceIdType.MESH)

    for other in others:
        greet(folds=other)

    @pl.when(has_left)
    def _():
        greet(samples=z - 1)

    @pl.when(has_right)
    def _():
        greet(samples=z + 1)

    def is_self(dz, dx, dc):
        return (dz == z) & (dx == x) & (dc == c)

    senders = []
    for k in range(own_count):
        for r in range(SHRINK_LEVELS):
            place = (c * own_count + k) * SHRINK_LEVELS + r
            for b in range(blocks):
                senders.append((place // cores, b, lax.rem(place, cores), k, r))
    for sz, b, sc, k, r in senders:
        @pl.when(~is_self(sz, b, sc))
        def _():
            greet(samples=sz, blocks=b, folds=sc)

    targets = [(t, b) for t in range(chips) for b in range(blocks)]

    stack[...] = jnp.zeros_like(stack)
    total[...] = jnp.zeros_like(total)
    for load in loads:
        load.wait()
    stack[0:variants, :] = geno_ref[...]
    stack[size:size + traits, :] = trait_ref[...]
    label = label_ref[...]
    fold_row = lax.broadcasted_iota(jnp.int32, (16, width), 0)
    is_fold = fold_row == label
    earlier = lax.broadcasted_iota(jnp.int32, (width, width), 0) < lax.broadcasted_iota(
        jnp.int32, (width, width), 1
    )
    rank = jnp.dot(
        is_fold.astype(jnp.bfloat16), earlier.astype(jnp.bfloat16), preferred_element_type=jnp.float32
    )
    rank = jnp.sum(jnp.where(is_fold, rank, 0.0), axis=0, keepdims=True)
    target = rank + (label * rows_fold).astype(jnp.float32)
    places = lax.broadcasted_iota(jnp.int32, (width, width), 0).astype(jnp.float32)
    permute = (places == target).astype(jnp.bfloat16)
    ordered = dot_nt(stack[...], permute).astype(jnp.bfloat16)
    for q in range(FOLDS):
        for f in range(cores):
            land[z, q, f] = ordered[f * part:(f + 1) * part, q * rows_fold:(q + 1) * rows_fold]

    expected = len(others) + has_left.astype(jnp.int32) + has_right.astype(jnp.int32)
    farther = len(targets) - (goal == c).astype(jnp.int32)
    pl.semaphore_wait(barrier, expected + jnp.where(reports, farther, 0))

    def along(source, q, to, send):
        piece = land.at[source, q, c]
        return pltpu.make_async_remote_copy(
            src_ref=piece, dst_ref=piece, send_sem=send, recv_sem=next_recv.at[source, q],
            device_id={"samples": to}, device_id_type=pl.DeviceIdType.MESH,
        )

    def across(source, q, o):
        piece = land.at[source, q, c]
        return pltpu.make_async_remote_copy(
            src_ref=piece, dst_ref=piece, send_sem=side_sem.at[source, q, o],
            recv_sem=side_recv.at[source, q, o],
            device_id={"folds": others[o]}, device_id_type=pl.DeviceIdType.MESH,
        )

    def own_chunk(q, to_right):
        n, to = (0, z + 1) if to_right else (1, z - 1)
        return along(z, q, to, own_sem.at[n, q])

    for q_right, q_left in zip(early_right, early_left):
        @pl.when(has_right)
        def _():
            own_chunk(q_right, True).start()

        @pl.when(has_left)
        def _():
            own_chunk(q_left, False).start()

    def add(source, chunks):
        columns = []
        for q in chunks:
            piece = jnp.concatenate([land[source, q, f] for f in range(cores)], axis=0)
            columns.append(jnp.where(fold == q, jnp.zeros_like(piece), piece))
        both = jnp.concatenate(columns, axis=1)
        total[...] += dot_nt(both, both[0:size, :])

    add(z, range(FOLDS))

    def each_side(distance, fn):
        @pl.when(z - distance >= 0)
        def _():
            fn(z - distance, z + 1, has_right, early_right, last_right)

        @pl.when(z + distance < chips)
        def _():
            fn(z + distance, z - 1, has_left, early_left, last_left)

    def pass_on(source, q, onward, more):
        along(source, q, z, next_sem.at[source, q]).wait_recv()

        @pl.when(more)
        def _():
            along(source, q, onward, next_sem.at[source, q]).start()

        for o in range(cores - 1):
            across(source, q, o).start()

    def collect(source, onward, more, early, last):
        for q in early:
            for o in range(cores - 1):
                across(source, q, o).wait_recv()
        add(source, early)

    def receive(distance, carry):
        for n in range(FOLDS - 1):
            each_side(distance, lambda source, onward, more, early, last: pass_on(source, early[n], onward, more))

        @pl.when((z == distance) & has_right)
        def _():
            own_chunk(last_right, True).start()

        @pl.when((z + distance == chips - 1) & has_left)
        def _():
            own_chunk(last_left, False).start()

        @pl.when(distance > 1)
        def _():
            each_side(distance - 1, collect)

        return carry

    @pl.when(~has_left & has_right)
    def _():
        own_chunk(last_right, True).start()

    @pl.when(~has_right & has_left)
    def _():
        own_chunk(last_left, False).start()

    lax.fori_loop(1, chips, receive, 0)

    def idle(more, last):
        return ~more & (fold == last)

    def receive_last(distance, carry):
        def relay(source, onward, more, early, last):
            @pl.when(~idle(more, last))
            def _():
                pass_on(source, last, onward, more)

        each_side(distance, relay)
        return carry

    def collect_last(distance, carry):
        def collect_one(source, onward, more, early, last):
            @pl.when(~idle(more, last))
            def _():
                for o in range(cores - 1):
                    across(source, last, o).wait_recv()
                add(source, [last])

        each_side(distance, collect_one)
        return carry

    lax.fori_loop(1, chips, receive_last, 0)
    if chips > 1:
        each_side(chips - 1, collect)
    lax.fori_loop(1, chips, collect_last, 0)

    def late():
        def step(distance, carry):
            def relay(source, onward, more, early, last):
                @pl.when(idle(more, last))
                def _():
                    pass_on(source, last, onward, more)

            each_side(distance, relay)
            return carry

        lax.fori_loop(1, chips, step, 0)

    sub = lax.broadcasted_iota(jnp.int32, (size, size), 0)
    lane = lax.broadcasted_iota(jnp.int32, (size, size), 1)
    value = jnp.where(level == 0, value_ref[0], value_ref[SHRINK_LEVELS - 1])
    for r in range(1, SHRINK_LEVELS - 1):
        value = jnp.where(level == r, value_ref[r], value)
    added = jnp.where(sub == lane, jnp.where(sub < variants, value, 1.0), 0.0)
    total[...] = total[...] * (1.0 / tally)
    total[0:size, :] = total[0:size, :] + added
    work[...] = total[0:size, :]
    invert(work, strip, late)
    right = total[size:, :]
    inverse = split(work[...])
    first = rows_times(right, inverse)
    residual = right - rows_times(first, split(total[0:size, :]))
    betas = (first + rows_times(residual, inverse)).astype(jnp.bfloat16)

    def late_done(distance, carry):
        def wait(source, onward, more, early, last):
            @pl.when(idle(more, last))
            def _():
                for o in range(cores - 1):
                    across(source, last, o).wait_recv()

        each_side(distance, wait)
        return carry

    lax.fori_loop(1, chips, late_done, 0)
    for s in range(chips):
        chunk = jnp.concatenate([land[s, fold, f] for f in range(cores)], axis=0)
        preds = jnp.dot(betas, chunk[0:size, :], preferred_element_type=jnp.float32)
        preds_ref[:, s * rows_fold:(s + 1) * rows_fold] = preds.astype(jnp.bfloat16)

    def message(n, t, b):
        return pltpu.make_async_remote_copy(
            src_ref=preds_ref, dst_ref=slots.at[local, x, level], send_sem=send_sem.at[n],
            recv_sem=recv_sem.at[local, x, level],
            device_id={"samples": t, "blocks": b, "folds": goal}, device_id_type=pl.DeviceIdType.MESH,
        )

    @pl.when(reports)
    def _():
        for n, (t, b) in enumerate(targets):
            @pl.when(~is_self(t, b, goal))
            def _():
                message(n, t, b).start()

        @pl.when(goal == c)
        def _():
            slots[local, x, level] = preds_ref[...]

    for sz, b, sc, k, r in senders:
        @pl.when(~is_self(sz, b, sc))
        def _():
            piece = slots.at[k, b, r]
            pltpu.make_async_remote_copy(
                src_ref=piece, dst_ref=piece, send_sem=send_sem.at[0], recv_sem=recv_sem.at[k, b, r],
                device_id={"samples": sz}, device_id_type=pl.DeviceIdType.MESH,
            ).wait_recv()

    rows = slots.shape[3]

    def same_trait(mine, theirs):
        found = dot_nt(mine, theirs)
        at = lax.broadcasted_iota(jnp.int32, found.shape, 0)
        other = lax.rem(lax.broadcasted_iota(jnp.int32, found.shape, 1), rows)
        return jnp.sum(jnp.where(at == other, found, 0.0), axis=0, keepdims=True) / held

    for k in range(own_count):
        pieces = []
        for s in range(chips):
            chunk = jnp.concatenate([land[s, c * own_count + k, f] for f in range(cores)], axis=0)
            pieces.append(chunk[size:, :])
        trait = jnp.concatenate(pieces, axis=1)
        everything = jnp.concatenate(
            [slots[k, b, s] for b in range(blocks) for s in range(SHRINK_LEVELS)], axis=0
        )
        for r in range(SHRINK_LEVELS):
            mine = slots[k, x, r]
            out_ref[k, 0, r] = slots[k, x, r, 0:traits, pl.ds(pl.multiple_of(z * rows_fold, rows_fold), rows_fold)]
            found = same_trait(mine, everything)
            for b in range(blocks):
                for s in range(SHRINK_LEVELS):
                    start = (b * SHRINK_LEVELS + s) * rows
                    gram_ref[k, 0, r, b, s:s + 1, :] = found[:, start:start + traits]
            cross_ref[k, 0, r:r + 1, :] = same_trait(mine, trait)[:, 0:traits]

    @pl.when(reports)
    def _():
        for n, (t, b) in enumerate(targets):
            @pl.when(~is_self(t, b, goal))
            def _():
                message(n, t, b).wait_send()

    for q in range(FOLDS):
        @pl.when(has_right)
        def _():
            own_chunk(q, True).wait_send()

        @pl.when(has_left)
        def _():
            own_chunk(q, False).wait_send()

    def finish(distance, carry):
        def sent(source, onward, more, early, last):
            for q in range(FOLDS):
                @pl.when(more)
                def _():
                    along(source, q, onward, next_sem.at[source, q]).wait_send()

                for o in range(cores - 1):
                    across(source, q, o).wait_send()

        each_side(distance, sent)
        return carry

    lax.fori_loop(1, chips, finish, 0)


def per_device(allele_dosage_table, phenotype_values, individual_partition_label, shrink_strengths):
    chips, cores, blocks = lax.axis_size("samples"), lax.axis_size("folds"), lax.axis_size("blocks")
    variants, width = allele_dosage_table.shape
    traits = phenotype_values.shape[0]
    size = padded(variants, PANEL)
    rows = padded(size + padded(traits, 16), 16 * cores)
    part = rows // cores
    rows_fold = width // FOLDS
    held = chips * rows_fold
    own_count = FOLDS // cores
    vmem = pl.BlockSpec(memory_space=pltpu.VMEM)
    hbm = pl.BlockSpec(memory_space=pltpu.HBM)
    buffers = 2 * chips * (FOLDS * rows * rows_fold + own_count * blocks * SHRINK_LEVELS * (rows - size) * rows_fold)
    predictions, level_gram, level_cross = pl.pallas_call(
        functools.partial(kernel, (chips, cores, blocks, variants, size, traits, part)),
        out_shape=(
            jax.ShapeDtypeStruct((own_count, 1, SHRINK_LEVELS, traits, rows_fold), jnp.bfloat16),
            jax.ShapeDtypeStruct(
                (own_count, 1, SHRINK_LEVELS, blocks, SHRINK_LEVELS, traits), jnp.float32
            ),
            jax.ShapeDtypeStruct((own_count, 1, SHRINK_LEVELS, traits), jnp.float32),
        ),
        in_specs=[hbm, hbm, hbm, pl.BlockSpec(memory_space=pltpu.SMEM)],
        out_specs=(vmem,) * 3,
        scratch_shapes=[
            pltpu.VMEM((variants, width), jnp.bfloat16),
            pltpu.VMEM((traits, width), jnp.bfloat16),
            pltpu.VMEM((1, width), jnp.int32),
            pltpu.VMEM((rows, width), jnp.bfloat16),
            pltpu.VMEM((chips, FOLDS, cores, part, rows_fold), jnp.bfloat16),
            pltpu.VMEM((rows, size), jnp.float32),
            pltpu.VMEM((size, size), jnp.float32),
            pltpu.VMEM((PANEL, size), jnp.float32),
            pltpu.VMEM((rows - size, held), jnp.bfloat16),
            pltpu.VMEM((own_count, blocks, SHRINK_LEVELS, rows - size, held), jnp.bfloat16),
            pltpu.SemaphoreType.DMA((3,)),
            pltpu.SemaphoreType.DMA((2, FOLDS)),
            pltpu.SemaphoreType.DMA((chips, FOLDS)),
            pltpu.SemaphoreType.DMA((chips, FOLDS)),
            pltpu.SemaphoreType.DMA((chips, FOLDS, cores - 1)),
            pltpu.SemaphoreType.DMA((chips, FOLDS, cores - 1)),
            pltpu.SemaphoreType.DMA((chips * blocks,)),
            pltpu.SemaphoreType.DMA((own_count, blocks, SHRINK_LEVELS)),
        ],
        compiler_params=pltpu.CompilerParams(
            collective_id=0, has_side_effects=True, vmem_limit_bytes=buffers + 20 * 1024 * 1024
        ),
    )(allele_dosage_table, phenotype_values, individual_partition_label.reshape(1, width), shrink_strengths)
    level_gram = jnp.transpose(level_gram, (0, 1, 2, 5, 3, 4))
    return (predictions, level_gram, level_cross)


def solution(mesh):
    in_specs = (
        P("blocks", ("groups", "samples")),
        P(None, ("groups", "samples")),
        P(("groups", "samples")),
        P(),
    )
    out_specs = (
        P("folds", "blocks", None, None, ("groups", "samples")),
        P(("groups", "folds"), "blocks", None, None, None, None),
        P(("groups", "folds"), "blocks", None, None),
    )
    return jax.shard_map(
        per_device, mesh=mesh, in_specs=in_specs, out_specs=out_specs, check_vma=False
    )
```

```python
import functools

import jax
import jax.numpy as jnp
from jax import lax
from jax.experimental import pallas as pl
from jax.experimental.pallas import tpu as pltpu
from jax.sharding import PartitionSpec as P

SHRINK_LEVELS = 2
FOLDS = 4
PANEL = 128
MINI = 32


def split(a):
    high = a.astype(jnp.bfloat16)
    rest = a - high.astype(jnp.float32)
    mid = rest.astype(jnp.bfloat16)
    low = (rest - mid.astype(jnp.float32)).astype(jnp.bfloat16)
    return high, mid, low


def dot_f32(a, b, a_dim=1):
    ah, am, al = split(a)
    bh, bm, bl = split(b)
    left = jnp.concatenate([ah, ah, am, am, ah, al], axis=a_dim)
    right = jnp.concatenate([bh, bm, bh, bm, bl, bh], axis=0)
    return lax.dot_general(
        left, right, (((a_dim,), (0,)), ((), ())), preferred_element_type=jnp.float32
    )


def rows_times(a, parts):
    count = a.shape[0]
    stacked = jnp.concatenate(split(a), axis=0)
    total = None
    for n, part in enumerate(parts):
        found = jnp.dot(stacked[0:(3 - n) * count, :], part, preferred_element_type=jnp.float32)
        for i in range(3 - n):
            one = found[i * count:(i + 1) * count, :]
            total = one if total is None else total + one
    return total


def sweep(block, m):
    low = m * MINI
    size = block.shape[0]
    rows = block[low:low + MINI, :]
    lane = lax.broadcasted_iota(jnp.int32, (MINI, size), 1)
    sub = lax.broadcasted_iota(jnp.int32, (MINI, size), 0)
    inside = (lane >= low) & (lane < low + MINI)
    cols = [jnp.broadcast_to(rows[:, low + j:low + j + 1], (MINI, size)) for j in range(MINI)]
    run = jnp.where(inside, jnp.where(lane - low == sub, 1.0, 0.0), rows)
    scale = jnp.zeros((MINI, size), jnp.float32)
    for j in range(MINI):
        inv = 1.0 / cols[j][j:j + 1, :]
        here = sub == j
        scale = jnp.where(here, inv, scale)
        ratio = jnp.where(here, 0.0, cols[j]) * inv
        run = run - ratio * run[j:j + 1, :]
        for i in range(j + 1, MINI):
            cols[i] = cols[i] - ratio * cols[i][j:j + 1, :]
    run = run * scale
    turned = jnp.where(inside, 0.0, jnp.where(lane < low, -rows, rows))
    update = dot_f32(turned, run, a_dim=0)

    def outside(start, stop):
        lane = lax.broadcasted_iota(jnp.int32, (stop - start, size), 1)
        kept = jnp.where((lane >= low) & (lane < low + MINI), 0.0, block[start:stop, :])
        return kept - update[start:stop, :]

    parts = []
    if low:
        parts.append(outside(0, low))
    parts.append(run)
    if low + MINI < size:
        parts.append(outside(low + MINI, size))
    return jnp.concatenate(parts, axis=0)


def invert(work, strip, during):
    size = work.shape[0]

    def panel(p, carry):
        @pl.when(p == size // PANEL - 1)
        def _():
            during()

        off = pl.multiple_of(p * PANEL, PANEL)
        here = pl.ds(off, PANEL)
        block = work[here, here]
        for m in range(PANEL // MINI):
            block = sweep(block, m)
        sub = lax.broadcasted_iota(jnp.int32, (size, PANEL), 0)
        col = jnp.where((sub >= off) & (sub < off + PANEL), 0.0, work[:, here])
        work[:, here] = jnp.zeros((size, PANEL), jnp.float32)
        strip[...] = dot_f32(block, work[here, :])
        strip[:, here] = block
        work[...] = work[...] - dot_f32(col, strip[...])
        work[here, :] = strip[...]
        return carry

    lax.fori_loop(0, size // PANEL, panel, 0)


def padded(count, multiple):
    return (count + multiple - 1) // multiple * multiple


def dot_nt(a, b):
    return lax.dot_general(a, b, (((1,), (1,)), ((), ())), preferred_element_type=jnp.float32)


def own_pair(total_pairs):
    place = lax.axis_index("samples") * lax.axis_size("folds") + lax.axis_index("folds")
    return lax.rem(place, total_pairs), place < total_pairs


def kernel(shape, geno_hbm, trait_hbm, label_hbm, value_ref, out_ref, gram_ref, cross_ref,
           geno_ref, trait_ref, label_ref, stack, land, total, work, strip, preds_ref, slots,
           load_sem, own_sem, next_sem, next_recv, side_sem, side_recv, send_sem, recv_sem):
    chips, cores, blocks, variants, size, traits, part = shape
    z = lax.axis_index("samples")
    c = lax.axis_index("folds")
    x = lax.axis_index("blocks")
    width = stack.shape[1]
    rows_fold = width // FOLDS
    held = chips * rows_fold
    tally = chips * width - held
    own_count = FOLDS // cores
    pairs = FOLDS * SHRINK_LEVELS
    pair, reports = own_pair(pairs)
    fold, level = pair // SHRINK_LEVELS, lax.rem(pair, SHRINK_LEVELS)
    goal = fold // own_count
    local = lax.rem(fold, own_count)
    others = [lax.rem(c + o, cores) for o in range(1, cores)]
    has_left, has_right = z > 0, z < chips - 1
    last_right = ((chips - 1) * cores % pairs) // SHRINK_LEVELS
    last_left = 0
    early_right = [q for q in range(FOLDS) if q != last_right]
    early_left = [q for q in range(FOLDS) if q != last_left]

    loads = [
        pltpu.make_async_copy(source, goal_ref, load_sem.at[n])
        for n, (source, goal_ref) in enumerate(
            [(label_hbm, label_ref), (geno_hbm, geno_ref), (trait_hbm, trait_ref)]
        )
    ]
    for load in loads:
        load.start()

    barrier = pltpu.get_barrier_semaphore()

    def greet(**place):
        pl.semaphore_signal(barrier, inc=1, device_id=place, device_id_type=pl.DeviceIdType.MESH)

    for other in others:
        greet(folds=other)

    @pl.when(has_left)
    def _():
        greet(samples=z - 1)

    @pl.when(has_right)
    def _():
        greet(samples=z + 1)

    def is_self(dz, dx, dc):
        return (dz == z) & (dx == x) & (dc == c)

    senders = []
    for k in range(own_count):
        for r in range(SHRINK_LEVELS):
            place = (c * own_count + k) * SHRINK_LEVELS + r
            for b in range(blocks):
                senders.append((place // cores, b, lax.rem(place, cores), k, r))
    for sz, b, sc, k, r in senders:
        @pl.when(~is_self(sz, b, sc))
        def _():
            greet(samples=sz, blocks=b, folds=sc)

    targets = [(t, b) for t in range(chips) for b in range(blocks)]

    stack[...] = jnp.zeros_like(stack)
    total[...] = jnp.zeros_like(total)
    for load in loads:
        load.wait()
    stack[0:variants, :] = geno_ref[...]
    stack[size:size + traits, :] = trait_ref[...]
    label = label_ref[...]
    fold_row = lax.broadcasted_iota(jnp.int32, (16, width), 0)
    is_fold = fold_row == label
    earlier = lax.broadcasted_iota(jnp.int32, (width, width), 0) < lax.broadcasted_iota(
        jnp.int32, (width, width), 1
    )
    rank = jnp.dot(
        is_fold.astype(jnp.bfloat16), earlier.astype(jnp.bfloat16), preferred_element_type=jnp.float32
    )
    rank = jnp.sum(jnp.where(is_fold, rank, 0.0), axis=0, keepdims=True)
    target = rank + (label * rows_fold).astype(jnp.float32)
    places = lax.broadcasted_iota(jnp.int32, (width, width), 0).astype(jnp.float32)
    permute = (places == target).astype(jnp.bfloat16)
    ordered = dot_nt(stack[...], permute).astype(jnp.bfloat16)
    for q in range(FOLDS):
        for f in range(cores):
            land[z, q, f] = ordered[f * part:(f + 1) * part, q * rows_fold:(q + 1) * rows_fold]

    expected = len(others) + has_left.astype(jnp.int32) + has_right.astype(jnp.int32)
    farther = len(targets) - (goal == c).astype(jnp.int32)
    pl.semaphore_wait(barrier, expected + jnp.where(reports, farther, 0))

    def along(source, q, to, send):
        piece = land.at[source, q, c]
        return pltpu.make_async_remote_copy(
            src_ref=piece, dst_ref=piece, send_sem=send, recv_sem=next_recv.at[source, q],
            device_id={"samples": to}, device_id_type=pl.DeviceIdType.MESH,
        )

    def across(source, q, o):
        piece = land.at[source, q, c]
        return pltpu.make_async_remote_copy(
            src_ref=piece, dst_ref=piece, send_sem=side_sem.at[source, q, o],
            recv_sem=side_recv.at[source, q, o],
            device_id={"folds": others[o]}, device_id_type=pl.DeviceIdType.MESH,
        )

    def own_chunk(q, to_right):
        n, to = (0, z + 1) if to_right else (1, z - 1)
        return along(z, q, to, own_sem.at[n, q])

    for q_right, q_left in zip(early_right, early_left):
        @pl.when(has_right)
        def _():
            own_chunk(q_right, True).start()

        @pl.when(has_left)
        def _():
            own_chunk(q_left, False).start()

    def add(source, chunks):
        columns = []
        for q in chunks:
            piece = jnp.concatenate([land[source, q, f] for f in range(cores)], axis=0)
            columns.append(jnp.where(fold == q, jnp.zeros_like(piece), piece))
        both = jnp.concatenate(columns, axis=1)
        total[...] += dot_nt(both, both[0:size, :])

    add(z, range(FOLDS))

    def each_side(distance, fn):
        @pl.when(z - distance >= 0)
        def _():
            fn(z - distance, z + 1, has_right, early_right, last_right)

        @pl.when(z + distance < chips)
        def _():
            fn(z + distance, z - 1, has_left, early_left, last_left)

    def pass_on(source, q, onward, more):
        along(source, q, z, next_sem.at[source, q]).wait_recv()

        @pl.when(more)
        def _():
            along(source, q, onward, next_sem.at[source, q]).start()

        for o in range(cores - 1):
            across(source, q, o).start()

    def collect(source, onward, more, early, last):
        for q in early:
            for o in range(cores - 1):
                across(source, q, o).wait_recv()
        add(source, early)

    def receive(distance, carry):
        for n in range(FOLDS - 1):
            each_side(distance, lambda source, onward, more, early, last: pass_on(source, early[n], onward, more))

        @pl.when((z == distance) & has_right)
        def _():
            own_chunk(last_right, True).start()

        @pl.when((z + distance == chips - 1) & has_left)
        def _():
            own_chunk(last_left, False).start()

        @pl.when(distance > 1)
        def _():
            each_side(distance - 1, collect)

        return carry

    @pl.when(~has_left & has_right)
    def _():
        own_chunk(last_right, True).start()

    @pl.when(~has_right & has_left)
    def _():
        own_chunk(last_left, False).start()

    lax.fori_loop(1, chips, receive, 0)

    def idle(more, last):
        return ~more & (fold == last)

    def receive_last(distance, carry):
        def relay(source, onward, more, early, last):
            @pl.when(~idle(more, last))
            def _():
                pass_on(source, last, onward, more)

        each_side(distance, relay)
        return carry

    def collect_last(distance, carry):
        def collect_one(source, onward, more, early, last):
            @pl.when(~idle(more, last))
            def _():
                for o in range(cores - 1):
                    across(source, last, o).wait_recv()
                add(source, [last])

        each_side(distance, collect_one)
        return carry

    lax.fori_loop(1, chips, receive_last, 0)
    if chips > 1:
        each_side(chips - 1, collect)
    lax.fori_loop(1, chips, collect_last, 0)

    def late():
        def step(distance, carry):
            def relay(source, onward, more, early, last):
                @pl.when(idle(more, last))
                def _():
                    pass_on(source, last, onward, more)

            each_side(distance, relay)
            return carry

        lax.fori_loop(1, chips, step, 0)

    sub = lax.broadcasted_iota(jnp.int32, (size, size), 0)
    lane = lax.broadcasted_iota(jnp.int32, (size, size), 1)
    value = jnp.where(level == 0, value_ref[0], value_ref[SHRINK_LEVELS - 1])
    for r in range(1, SHRINK_LEVELS - 1):
        value = jnp.where(level == r, value_ref[r], value)
    added = jnp.where(sub == lane, jnp.where(sub < variants, value, 1.0), 0.0)
    total[...] = total[...] * (1.0 / tally)
    total[0:size, :] = total[0:size, :] + added
    work[...] = total[0:size, :]
    invert(work, strip, late)
    right = total[size:, :]
    inverse = split(work[...])
    first = rows_times(right, inverse)
    residual = right - rows_times(first, split(total[0:size, :]))
    betas = (first + rows_times(residual, inverse)).astype(jnp.bfloat16)

    def late_done(distance, carry):
        def wait(source, onward, more, early, last):
            @pl.when(idle(more, last))
            def _():
                for o in range(cores - 1):
                    across(source, last, o).wait_recv()

        each_side(distance, wait)
        return carry

    lax.fori_loop(1, chips, late_done, 0)
    for s in range(chips):
        chunk = jnp.concatenate([land[s, fold, f] for f in range(cores)], axis=0)
        preds = jnp.dot(betas, chunk[0:size, :], preferred_element_type=jnp.float32)
        preds_ref[:, s * rows_fold:(s + 1) * rows_fold] = preds.astype(jnp.bfloat16)

    def message(n, t, b):
        return pltpu.make_async_remote_copy(
            src_ref=preds_ref, dst_ref=slots.at[local, x, level], send_sem=send_sem.at[n],
            recv_sem=recv_sem.at[local, x, level],
            device_id={"samples": t, "blocks": b, "folds": goal}, device_id_type=pl.DeviceIdType.MESH,
        )

    @pl.when(reports)
    def _():
        for n, (t, b) in enumerate(targets):
            @pl.when(~is_self(t, b, goal))
            def _():
                message(n, t, b).start()

        @pl.when(goal == c)
        def _():
            slots[local, x, level] = preds_ref[...]

    for sz, b, sc, k, r in senders:
        @pl.when(~is_self(sz, b, sc))
        def _():
            piece = slots.at[k, b, r]
            pltpu.make_async_remote_copy(
                src_ref=piece, dst_ref=piece, send_sem=send_sem.at[0], recv_sem=recv_sem.at[k, b, r],
                device_id={"samples": sz}, device_id_type=pl.DeviceIdType.MESH,
            ).wait_recv()

    rows = slots.shape[3]

    def same_trait(mine, theirs):
        found = dot_nt(mine, theirs)
        at = lax.broadcasted_iota(jnp.int32, found.shape, 0)
        other = lax.rem(lax.broadcasted_iota(jnp.int32, found.shape, 1), rows)
        return jnp.sum(jnp.where(at == other, found, 0.0), axis=0, keepdims=True) / held

    for k in range(own_count):
        pieces = []
        for s in range(chips):
            chunk = jnp.concatenate([land[s, c * own_count + k, f] for f in range(cores)], axis=0)
            pieces.append(chunk[size:, :])
        trait = jnp.concatenate(pieces, axis=1)
        everything = jnp.concatenate(
            [slots[k, b, s] for b in range(blocks) for s in range(SHRINK_LEVELS)], axis=0
        )
        for r in range(SHRINK_LEVELS):
            mine = slots[k, x, r]
            out_ref[k, 0, r] = slots[k, x, r, 0:traits, pl.ds(pl.multiple_of(z * rows_fold, rows_fold), rows_fold)]
            found = same_trait(mine, everything)
            for b in range(blocks):
                for s in range(SHRINK_LEVELS):
                    start = (b * SHRINK_LEVELS + s) * rows
                    gram_ref[k, 0, r, b, s:s + 1, :] = found[:, start:start + traits]
            cross_ref[k, 0, r:r + 1, :] = same_trait(mine, trait)[:, 0:traits]

    @pl.when(reports)
    def _():
        for n, (t, b) in enumerate(targets):
            @pl.when(~is_self(t, b, goal))
            def _():
                message(n, t, b).wait_send()

    for q in range(FOLDS):
        @pl.when(has_right)
        def _():
            own_chunk(q, True).wait_send()

        @pl.when(has_left)
        def _():
            own_chunk(q, False).wait_send()

    def finish(distance, carry):
        def sent(source, onward, more, early, last):
            for q in range(FOLDS):
                @pl.when(more)
                def _():
                    along(source, q, onward, next_sem.at[source, q]).wait_send()

                for o in range(cores - 1):
                    across(source, q, o).wait_send()

        each_side(distance, sent)
        return carry

    lax.fori_loop(1, chips, finish, 0)


def per_device(allele_dosage_table, phenotype_values, individual_partition_label, shrink_strengths):
    chips, cores, blocks = lax.axis_size("samples"), lax.axis_size("folds"), lax.axis_size("blocks")
    variants, width = allele_dosage_table.shape
    traits = phenotype_values.shape[0]
    size = padded(variants, PANEL)
    rows = padded(size + padded(traits, 16), 16 * cores)
    part = rows // cores
    rows_fold = width // FOLDS
    held = chips * rows_fold
    own_count = FOLDS // cores
    vmem = pl.BlockSpec(memory_space=pltpu.VMEM)
    hbm = pl.BlockSpec(memory_space=pl.ANY)
    predictions, level_gram, level_cross = pl.pallas_call(
        functools.partial(kernel, (chips, cores, blocks, variants, size, traits, part)),
        out_shape=(
            jax.ShapeDtypeStruct((own_count, 1, SHRINK_LEVELS, traits, rows_fold), jnp.bfloat16),
            jax.ShapeDtypeStruct(
                (own_count, 1, SHRINK_LEVELS, blocks, SHRINK_LEVELS, traits), jnp.float32
            ),
            jax.ShapeDtypeStruct((own_count, 1, SHRINK_LEVELS, traits), jnp.float32),
        ),
        in_specs=[hbm, hbm, hbm, pl.BlockSpec(memory_space=pltpu.SMEM)],
        out_specs=(vmem,) * 3,
        scratch_shapes=[
            pltpu.VMEM((variants, width), jnp.bfloat16),
            pltpu.VMEM((traits, width), jnp.bfloat16),
            pltpu.VMEM((1, width), jnp.int32),
            pltpu.VMEM((rows, width), jnp.bfloat16),
            pltpu.VMEM((chips, FOLDS, cores, part, rows_fold), jnp.bfloat16),
            pltpu.VMEM((rows, size), jnp.float32),
            pltpu.VMEM((size, size), jnp.float32),
            pltpu.VMEM((PANEL, size), jnp.float32),
            pltpu.VMEM((rows - size, held), jnp.bfloat16),
            pltpu.VMEM((own_count, blocks, SHRINK_LEVELS, rows - size, held), jnp.bfloat16),
            pltpu.SemaphoreType.DMA((3,)),
            pltpu.SemaphoreType.DMA((2, FOLDS)),
            pltpu.SemaphoreType.DMA((chips, FOLDS)),
            pltpu.SemaphoreType.DMA((chips, FOLDS)),
            pltpu.SemaphoreType.DMA((chips, FOLDS, cores - 1)),
            pltpu.SemaphoreType.DMA((chips, FOLDS, cores - 1)),
            pltpu.SemaphoreType.DMA((chips * blocks,)),
            pltpu.SemaphoreType.DMA((own_count, blocks, SHRINK_LEVELS)),
        ],
        compiler_params=pltpu.CompilerParams(
            collective_id=0, has_side_effects=True, vmem_limit_bytes=60 * 1024 * 1024
        ),
    )(allele_dosage_table, phenotype_values, individual_partition_label.reshape(1, width), shrink_strengths)
    level_gram = jnp.transpose(level_gram, (0, 1, 2, 5, 3, 4))
    return (predictions, level_gram, level_cross)


def solution(mesh):
    in_specs = (
        P("blocks", ("groups", "samples")),
        P(None, ("groups", "samples")),
        P(("groups", "samples")),
        P(),
    )
    out_specs = (
        P("folds", "blocks", None, None, ("groups", "samples")),
        P(("groups", "folds"), "blocks", None, None, None, None),
        P(("groups", "folds"), "blocks", None, None),
    )
    return jax.shard_map(
        per_device, mesh=mesh, in_specs=in_specs, out_specs=out_specs, check_vma=False
    )
```

```python
import functools

import jax
import jax.numpy as jnp
from jax import lax
from jax.experimental import pallas as pl
from jax.experimental.pallas import tpu as pltpu
from jax.sharding import PartitionSpec as P

SHRINK_LEVELS = 2
FOLDS = 4
PANEL = 128
MINI = 16


def split(a):
    high = a.astype(jnp.bfloat16)
    rest = a - high.astype(jnp.float32)
    mid = rest.astype(jnp.bfloat16)
    low = (rest - mid.astype(jnp.float32)).astype(jnp.bfloat16)
    return high, mid, low


def dot_f32(a, b, a_dim=1):
    ah, am, al = split(a)
    bh, bm, bl = split(b)
    left = jnp.concatenate([ah, ah, am, am, ah, al], axis=a_dim)
    right = jnp.concatenate([bh, bm, bh, bm, bl, bh], axis=0)
    return lax.dot_general(
        left, right, (((a_dim,), (0,)), ((), ())), preferred_element_type=jnp.float32
    )


def rows_times(a, parts):
    count = a.shape[0]
    stacked = jnp.concatenate(split(a), axis=0)
    total = None
    for n, part in enumerate(parts):
        found = jnp.dot(stacked[0:(3 - n) * count, :], part, preferred_element_type=jnp.float32)
        for i in range(3 - n):
            one = found[i * count:(i + 1) * count, :]
            total = one if total is None else total + one
    return total


def sweep(block, m):
    low = m * MINI
    size = block.shape[0]
    rows = block[low:low + MINI, :]
    lane = lax.broadcasted_iota(jnp.int32, (MINI, size), 1)
    sub = lax.broadcasted_iota(jnp.int32, (MINI, size), 0)
    inside = (lane >= low) & (lane < low + MINI)
    cols = [jnp.broadcast_to(rows[:, low + j:low + j + 1], (MINI, size)) for j in range(MINI)]
    run = jnp.where(inside, jnp.where(lane - low == sub, 1.0, 0.0), rows)
    scale = jnp.zeros((MINI, size), jnp.float32)
    for j in range(MINI):
        inv = 1.0 / cols[j][j:j + 1, :]
        here = sub == j
        scale = jnp.where(here, inv, scale)
        ratio = jnp.where(here, 0.0, cols[j]) * inv
        run = run - ratio * run[j:j + 1, :]
        for i in range(j + 1, MINI):
            cols[i] = cols[i] - ratio * cols[i][j:j + 1, :]
    run = run * scale
    turned = jnp.where(inside, 0.0, jnp.where(lane < low, -rows, rows))
    update = dot_f32(turned, run, a_dim=0)

    def outside(start, stop):
        lane = lax.broadcasted_iota(jnp.int32, (stop - start, size), 1)
        kept = jnp.where((lane >= low) & (lane < low + MINI), 0.0, block[start:stop, :])
        return kept - update[start:stop, :]

    parts = []
    if low:
        parts.append(outside(0, low))
    parts.append(run)
    if low + MINI < size:
        parts.append(outside(low + MINI, size))
    return jnp.concatenate(parts, axis=0)


def invert_block(block):
    for m in range(PANEL // MINI):
        block = sweep(block, m)
    return block


def invert(work, strip, during):
    size = work.shape[0]
    panels = size // PANEL

    def panel(p, block, ahead):
        off = pl.multiple_of(p * PANEL, PANEL)
        here = pl.ds(off, PANEL)
        sub = lax.broadcasted_iota(jnp.int32, (size, PANEL), 0)
        col = jnp.where((sub >= off) & (sub < off + PANEL), 0.0, work[:, here])
        if ahead:
            then = pl.ds(pl.multiple_of(off + PANEL, PANEL), PANEL)
            above = work[here, then]
            following = work[then, then] - dot_f32(work[then, here], dot_f32(block, above))
        work[:, here] = jnp.zeros((size, PANEL), jnp.float32)
        strip[...] = dot_f32(block, work[here, :])
        strip[:, here] = block
        work[...] = work[...] - dot_f32(col, strip[...])
        work[here, :] = strip[...]
        return invert_block(following) if ahead else block

    def step(p, block):
        @pl.when(p == panels - 2)
        def _():
            during()

        return panel(p, block, True)

    block = lax.fori_loop(0, panels - 1, step, invert_block(work[0:PANEL, 0:PANEL]))
    if panels == 1:
        during()
    panel(panels - 1, block, False)


def padded(count, multiple):
    return (count + multiple - 1) // multiple * multiple


def dot_nt(a, b):
    return lax.dot_general(a, b, (((1,), (1,)), ((), ())), preferred_element_type=jnp.float32)


def own_pair(total_pairs):
    place = lax.axis_index("samples") * lax.axis_size("folds") + lax.axis_index("folds")
    return lax.rem(place, total_pairs), place < total_pairs


def kernel(shape, geno_hbm, trait_hbm, label_hbm, value_ref, out_ref, gram_ref, cross_ref,
           geno_ref, trait_ref, label_ref, stack, land, total, work, strip, preds_ref, slots,
           load_sem, own_sem, next_sem, next_recv, side_sem, side_recv, send_sem, recv_sem):
    chips, cores, blocks, variants, size, traits, part = shape
    z = lax.axis_index("samples")
    c = lax.axis_index("folds")
    x = lax.axis_index("blocks")
    width = stack.shape[1]
    rows_fold = width // FOLDS
    held = chips * rows_fold
    tally = chips * width - held
    own_count = FOLDS // cores
    pairs = FOLDS * SHRINK_LEVELS
    pair, reports = own_pair(pairs)
    fold, level = pair // SHRINK_LEVELS, lax.rem(pair, SHRINK_LEVELS)
    goal = fold // own_count
    local = lax.rem(fold, own_count)
    others = [lax.rem(c + o, cores) for o in range(1, cores)]
    has_left, has_right = z > 0, z < chips - 1
    last_right = ((chips - 1) * cores % pairs) // SHRINK_LEVELS
    last_left = 0
    early_right = [q for q in range(FOLDS) if q != last_right]
    early_left = [q for q in range(FOLDS) if q != last_left]

    loads = [
        pltpu.make_async_copy(source, goal_ref, load_sem.at[n])
        for n, (source, goal_ref) in enumerate(
            [(label_hbm, label_ref), (geno_hbm, geno_ref), (trait_hbm, trait_ref)]
        )
    ]
    for load in loads:
        load.start()

    barrier = pltpu.get_barrier_semaphore()

    def greet(**place):
        pl.semaphore_signal(barrier, inc=1, device_id=place, device_id_type=pl.DeviceIdType.MESH)

    for other in others:
        greet(folds=other)

    @pl.when(has_left)
    def _():
        greet(samples=z - 1)

    @pl.when(has_right)
    def _():
        greet(samples=z + 1)

    def is_self(dz, dx, dc):
        return (dz == z) & (dx == x) & (dc == c)

    senders = []
    for k in range(own_count):
        for r in range(SHRINK_LEVELS):
            place = (c * own_count + k) * SHRINK_LEVELS + r
            for b in range(blocks):
                senders.append((place // cores, b, lax.rem(place, cores), k, r))
    for sz, b, sc, k, r in senders:
        @pl.when(~is_self(sz, b, sc))
        def _():
            greet(samples=sz, blocks=b, folds=sc)

    targets = [(t, b) for t in range(chips) for b in range(blocks)]

    stack[...] = jnp.zeros_like(stack)
    total[...] = jnp.zeros_like(total)
    loads[0].wait()
    label = label_ref[...]
    fold_row = lax.broadcasted_iota(jnp.int32, (16, width), 0)
    is_fold = fold_row == label
    earlier = lax.broadcasted_iota(jnp.int32, (width, width), 0) < lax.broadcasted_iota(
        jnp.int32, (width, width), 1
    )
    rank = jnp.dot(
        is_fold.astype(jnp.bfloat16), earlier.astype(jnp.bfloat16), preferred_element_type=jnp.float32
    )
    rank = jnp.sum(jnp.where(is_fold, rank, 0.0), axis=0, keepdims=True)
    target = rank + (label * rows_fold).astype(jnp.float32)
    places = lax.broadcasted_iota(jnp.int32, (width, width), 0).astype(jnp.float32)
    permute = (places == target).astype(jnp.bfloat16)
    for load in loads[1:]:
        load.wait()
    stack[0:variants, :] = geno_ref[...]
    stack[size:size + traits, :] = trait_ref[...]
    ordered = dot_nt(stack[...], permute).astype(jnp.bfloat16)
    for q in range(FOLDS):
        for f in range(cores):
            land[z, q, f] = ordered[f * part:(f + 1) * part, q * rows_fold:(q + 1) * rows_fold]

    expected = len(others) + has_left.astype(jnp.int32) + has_right.astype(jnp.int32)
    farther = len(targets) - (goal == c).astype(jnp.int32)
    pl.semaphore_wait(barrier, expected + jnp.where(reports, farther, 0))

    def along(source, q, to, send):
        piece = land.at[source, q, c]
        return pltpu.make_async_remote_copy(
            src_ref=piece, dst_ref=piece, send_sem=send, recv_sem=next_recv.at[source, q],
            device_id={"samples": to}, device_id_type=pl.DeviceIdType.MESH,
        )

    def across(source, q, o):
        piece = land.at[source, q, c]
        return pltpu.make_async_remote_copy(
            src_ref=piece, dst_ref=piece, send_sem=side_sem.at[source, q, o],
            recv_sem=side_recv.at[source, q, o],
            device_id={"folds": others[o]}, device_id_type=pl.DeviceIdType.MESH,
        )

    def own_chunk(q, to_right):
        n, to = (0, z + 1) if to_right else (1, z - 1)
        return along(z, q, to, own_sem.at[n, q])

    for q_right, q_left in zip(early_right, early_left):
        @pl.when(has_right)
        def _():
            own_chunk(q_right, True).start()

        @pl.when(has_left)
        def _():
            own_chunk(q_left, False).start()

    def add(source, chunks):
        columns = []
        for q in chunks:
            piece = jnp.concatenate([land[source, q, f] for f in range(cores)], axis=0)
            columns.append(jnp.where(fold == q, jnp.zeros_like(piece), piece))
        both = jnp.concatenate(columns, axis=1)
        total[...] += dot_nt(both, both[0:size, :])

    add(z, range(FOLDS))

    def each_side(distance, fn):
        @pl.when(z - distance >= 0)
        def _():
            fn(z - distance, z + 1, has_right, early_right, last_right)

        @pl.when(z + distance < chips)
        def _():
            fn(z + distance, z - 1, has_left, early_left, last_left)

    def pass_on(source, q, onward, more):
        along(source, q, z, next_sem.at[source, q]).wait_recv()

        @pl.when(more)
        def _():
            along(source, q, onward, next_sem.at[source, q]).start()

        for o in range(cores - 1):
            across(source, q, o).start()

    def collect(source, onward, more, early, last):
        for q in early:
            for o in range(cores - 1):
                across(source, q, o).wait_recv()
        add(source, early)

    def receive(distance, carry):
        for n in range(FOLDS - 1):
            each_side(distance, lambda source, onward, more, early, last: pass_on(source, early[n], onward, more))

        @pl.when((z == distance) & has_right)
        def _():
            own_chunk(last_right, True).start()

        @pl.when((z + distance == chips - 1) & has_left)
        def _():
            own_chunk(last_left, False).start()

        @pl.when(distance > 1)
        def _():
            each_side(distance - 1, collect)

        return carry

    @pl.when(~has_left & has_right)
    def _():
        own_chunk(last_right, True).start()

    @pl.when(~has_right & has_left)
    def _():
        own_chunk(last_left, False).start()

    lax.fori_loop(1, chips, receive, 0)

    def idle(more, last):
        return ~more & (fold == last)

    def receive_last(distance, carry):
        def relay(source, onward, more, early, last):
            @pl.when(~idle(more, last))
            def _():
                pass_on(source, last, onward, more)

        each_side(distance, relay)
        return carry

    def collect_last(distance, carry):
        def collect_one(source, onward, more, early, last):
            @pl.when(~idle(more, last))
            def _():
                for o in range(cores - 1):
                    across(source, last, o).wait_recv()
                add(source, [last])

        each_side(distance, collect_one)
        return carry

    lax.fori_loop(1, chips, receive_last, 0)
    if chips > 1:
        each_side(chips - 1, collect)
    lax.fori_loop(1, chips, collect_last, 0)

    def late():
        def step(distance, carry):
            def relay(source, onward, more, early, last):
                @pl.when(idle(more, last))
                def _():
                    pass_on(source, last, onward, more)

            each_side(distance, relay)
            return carry

        lax.fori_loop(1, chips, step, 0)

    sub = lax.broadcasted_iota(jnp.int32, (size, size), 0)
    lane = lax.broadcasted_iota(jnp.int32, (size, size), 1)
    value = jnp.where(level == 0, value_ref[0], value_ref[SHRINK_LEVELS - 1])
    for r in range(1, SHRINK_LEVELS - 1):
        value = jnp.where(level == r, value_ref[r], value)
    added = jnp.where(sub == lane, jnp.where(sub < variants, value, 1.0), 0.0)
    total[...] = total[...] * (1.0 / tally)
    total[0:size, :] = total[0:size, :] + added
    work[...] = total[0:size, :]
    invert(work, strip, late)
    right = total[size:, :]
    inverse = split(work[...])
    first = rows_times(right, inverse)
    residual = right - rows_times(first, split(total[0:size, :]))
    betas = (first + rows_times(residual, inverse)).astype(jnp.bfloat16)

    def late_done(distance, carry):
        def wait(source, onward, more, early, last):
            @pl.when(idle(more, last))
            def _():
                for o in range(cores - 1):
                    across(source, last, o).wait_recv()

        each_side(distance, wait)
        return carry

    lax.fori_loop(1, chips, late_done, 0)
    for s in range(chips):
        chunk = jnp.concatenate([land[s, fold, f] for f in range(cores)], axis=0)
        preds = jnp.dot(betas, chunk[0:size, :], preferred_element_type=jnp.float32)
        preds_ref[:, s * rows_fold:(s + 1) * rows_fold] = preds.astype(jnp.bfloat16)

    def message(n, t, b):
        return pltpu.make_async_remote_copy(
            src_ref=preds_ref, dst_ref=slots.at[local, x, level], send_sem=send_sem.at[n],
            recv_sem=recv_sem.at[local, x, level],
            device_id={"samples": t, "blocks": b, "folds": goal}, device_id_type=pl.DeviceIdType.MESH,
        )

    @pl.when(reports)
    def _():
        for n, (t, b) in enumerate(targets):
            @pl.when(~is_self(t, b, goal))
            def _():
                message(n, t, b).start()

        @pl.when(goal == c)
        def _():
            slots[local, x, level] = preds_ref[...]

    for sz, b, sc, k, r in senders:
        @pl.when(~is_self(sz, b, sc))
        def _():
            piece = slots.at[k, b, r]
            pltpu.make_async_remote_copy(
                src_ref=piece, dst_ref=piece, send_sem=send_sem.at[0], recv_sem=recv_sem.at[k, b, r],
                device_id={"samples": sz}, device_id_type=pl.DeviceIdType.MESH,
            ).wait_recv()

    rows = slots.shape[3]

    def same_trait(mine, theirs):
        found = dot_nt(mine, theirs)
        at = lax.broadcasted_iota(jnp.int32, found.shape, 0)
        other = lax.rem(lax.broadcasted_iota(jnp.int32, found.shape, 1), rows)
        return jnp.sum(jnp.where(at == other, found, 0.0), axis=0, keepdims=True) / held

    for k in range(own_count):
        pieces = []
        for s in range(chips):
            chunk = jnp.concatenate([land[s, c * own_count + k, f] for f in range(cores)], axis=0)
            pieces.append(chunk[size:, :])
        trait = jnp.concatenate(pieces, axis=1)
        everything = jnp.concatenate(
            [slots[k, b, s] for b in range(blocks) for s in range(SHRINK_LEVELS)], axis=0
        )
        for r in range(SHRINK_LEVELS):
            mine = slots[k, x, r]
            out_ref[k, 0, r] = slots[k, x, r, 0:traits, pl.ds(pl.multiple_of(z * rows_fold, rows_fold), rows_fold)]
            found = same_trait(mine, everything)
            for b in range(blocks):
                for s in range(SHRINK_LEVELS):
                    start = (b * SHRINK_LEVELS + s) * rows
                    gram_ref[k, 0, r, b, s:s + 1, :] = found[:, start:start + traits]
            cross_ref[k, 0, r:r + 1, :] = same_trait(mine, trait)[:, 0:traits]

    @pl.when(reports)
    def _():
        for n, (t, b) in enumerate(targets):
            @pl.when(~is_self(t, b, goal))
            def _():
                message(n, t, b).wait_send()

    for q in range(FOLDS):
        @pl.when(has_right)
        def _():
            own_chunk(q, True).wait_send()

        @pl.when(has_left)
        def _():
            own_chunk(q, False).wait_send()

    def finish(distance, carry):
        def sent(source, onward, more, early, last):
            for q in range(FOLDS):
                @pl.when(more)
                def _():
                    along(source, q, onward, next_sem.at[source, q]).wait_send()

                for o in range(cores - 1):
                    across(source, q, o).wait_send()

        each_side(distance, sent)
        return carry

    lax.fori_loop(1, chips, finish, 0)


def per_device(allele_dosage_table, phenotype_values, individual_partition_label, shrink_strengths):
    chips, cores, blocks = lax.axis_size("samples"), lax.axis_size("folds"), lax.axis_size("blocks")
    variants, width = allele_dosage_table.shape
    traits = phenotype_values.shape[0]
    size = padded(variants, PANEL)
    rows = padded(size + padded(traits, 16), 16 * cores)
    part = rows // cores
    rows_fold = width // FOLDS
    held = chips * rows_fold
    own_count = FOLDS // cores
    vmem = pl.BlockSpec(memory_space=pltpu.VMEM)
    hbm = pl.BlockSpec(memory_space=pl.ANY)
    predictions, level_gram, level_cross = pl.pallas_call(
        functools.partial(kernel, (chips, cores, blocks, variants, size, traits, part)),
        out_shape=(
            jax.ShapeDtypeStruct((own_count, 1, SHRINK_LEVELS, traits, rows_fold), jnp.bfloat16),
            jax.ShapeDtypeStruct(
                (own_count, 1, SHRINK_LEVELS, blocks, SHRINK_LEVELS, traits), jnp.float32
            ),
            jax.ShapeDtypeStruct((own_count, 1, SHRINK_LEVELS, traits), jnp.float32),
        ),
        in_specs=[hbm, hbm, hbm, pl.BlockSpec(memory_space=pltpu.SMEM)],
        out_specs=(vmem,) * 3,
        scratch_shapes=[
            pltpu.VMEM((variants, width), jnp.bfloat16),
            pltpu.VMEM((traits, width), jnp.bfloat16),
            pltpu.VMEM((1, width), jnp.int32),
            pltpu.VMEM((rows, width), jnp.bfloat16),
            pltpu.VMEM((chips, FOLDS, cores, part, rows_fold), jnp.bfloat16),
            pltpu.VMEM((rows, size), jnp.float32),
            pltpu.VMEM((size, size), jnp.float32),
            pltpu.VMEM((PANEL, size), jnp.float32),
            pltpu.VMEM((rows - size, held), jnp.bfloat16),
            pltpu.VMEM((own_count, blocks, SHRINK_LEVELS, rows - size, held), jnp.bfloat16),
            pltpu.SemaphoreType.DMA((3,)),
            pltpu.SemaphoreType.DMA((2, FOLDS)),
            pltpu.SemaphoreType.DMA((chips, FOLDS)),
            pltpu.SemaphoreType.DMA((chips, FOLDS)),
            pltpu.SemaphoreType.DMA((chips, FOLDS, cores - 1)),
            pltpu.SemaphoreType.DMA((chips, FOLDS, cores - 1)),
            pltpu.SemaphoreType.DMA((chips * blocks,)),
            pltpu.SemaphoreType.DMA((own_count, blocks, SHRINK_LEVELS)),
        ],
        compiler_params=pltpu.CompilerParams(
            collective_id=0, has_side_effects=True, vmem_limit_bytes=60 * 1024 * 1024
        ),
    )(allele_dosage_table, phenotype_values, individual_partition_label.reshape(1, width), shrink_strengths)
    level_gram = jnp.transpose(level_gram, (0, 1, 2, 5, 3, 4))
    return (predictions, level_gram, level_cross)


def solution(mesh):
    in_specs = (
        P("blocks", ("groups", "samples")),
        P(None, ("groups", "samples")),
        P(("groups", "samples")),
        P(),
    )
    out_specs = (
        P("folds", "blocks", None, None, ("groups", "samples")),
        P(("groups", "folds"), "blocks", None, None, None, None),
        P(("groups", "folds"), "blocks", None, None),
    )
    return jax.shard_map(
        per_device, mesh=mesh, in_specs=in_specs, out_specs=out_specs, check_vma=False
    )
```

```python
import functools

import jax
import jax.numpy as jnp
from jax import lax
from jax.experimental import pallas as pl
from jax.experimental.pallas import tpu as pltpu
from jax.sharding import PartitionSpec as P

SHRINK_LEVELS = 2
FOLDS = 4
PANEL = 128
MINI = 16


def split(a):
    high = a.astype(jnp.bfloat16)
    rest = a - high.astype(jnp.float32)
    mid = rest.astype(jnp.bfloat16)
    low = (rest - mid.astype(jnp.float32)).astype(jnp.bfloat16)
    return high, mid, low


def dot_f32(a, b, a_dim=1):
    ah, am, al = split(a)
    bh, bm, bl = split(b)
    left = jnp.concatenate([ah, ah, am, am, ah, al], axis=a_dim)
    right = jnp.concatenate([bh, bm, bh, bm, bl, bh], axis=0)
    return lax.dot_general(
        left, right, (((a_dim,), (0,)), ((), ())), preferred_element_type=jnp.float32
    )


def rows_times(a, parts):
    count = a.shape[0]
    stacked = jnp.concatenate(split(a), axis=0)
    total = None
    for n, part in enumerate(parts):
        found = jnp.dot(stacked[0:(3 - n) * count, :], part, preferred_element_type=jnp.float32)
        for i in range(3 - n):
            one = found[i * count:(i + 1) * count, :]
            total = one if total is None else total + one
    return total


def sweep(block, m):
    low = m * MINI
    size = block.shape[0]
    rows = block[low:low + MINI, :]
    lane = lax.broadcasted_iota(jnp.int32, (MINI, size), 1)
    sub = lax.broadcasted_iota(jnp.int32, (MINI, size), 0)
    inside = (lane >= low) & (lane < low + MINI)
    cols = [jnp.broadcast_to(rows[:, low + j:low + j + 1], (MINI, size)) for j in range(MINI)]
    run = jnp.where(inside, jnp.where(lane - low == sub, 1.0, 0.0), rows)
    scale = jnp.zeros((MINI, size), jnp.float32)
    for j in range(MINI):
        pivot = cols[j][j:j + 1, :]
        inv = pl.reciprocal(pivot, approx=True)
        for _ in range(2):
            inv = inv * (2.0 - pivot * inv)
        here = sub == j
        scale = jnp.where(here, inv, scale)
        ratio = jnp.where(here, 0.0, cols[j]) * inv
        run = run - ratio * run[j:j + 1, :]
        for i in range(j + 1, MINI):
            cols[i] = cols[i] - ratio * cols[i][j:j + 1, :]
    run = run * scale
    turned = jnp.where(inside, 0.0, jnp.where(lane < low, -rows, rows))
    update = dot_f32(turned, run, a_dim=0)

    def outside(start, stop):
        lane = lax.broadcasted_iota(jnp.int32, (stop - start, size), 1)
        kept = jnp.where((lane >= low) & (lane < low + MINI), 0.0, block[start:stop, :])
        return kept - update[start:stop, :]

    parts = []
    if low:
        parts.append(outside(0, low))
    parts.append(run)
    if low + MINI < size:
        parts.append(outside(low + MINI, size))
    return jnp.concatenate(parts, axis=0)


def invert_block(block):
    for m in range(PANEL // MINI):
        block = sweep(block, m)
    return block


def invert(work, strip, during):
    size = work.shape[0]
    panels = size // PANEL

    def panel(p, block, ahead):
        off = pl.multiple_of(p * PANEL, PANEL)
        here = pl.ds(off, PANEL)
        sub = lax.broadcasted_iota(jnp.int32, (size, PANEL), 0)
        col = jnp.where((sub >= off) & (sub < off + PANEL), 0.0, work[:, here])
        if ahead:
            then = pl.ds(pl.multiple_of(off + PANEL, PANEL), PANEL)
            above = work[here, then]
            following = work[then, then] - dot_f32(work[then, here], dot_f32(block, above))
        work[:, here] = jnp.zeros((size, PANEL), jnp.float32)
        strip[...] = dot_f32(block, work[here, :])
        strip[:, here] = block
        work[...] = work[...] - dot_f32(col, strip[...])
        work[here, :] = strip[...]
        return invert_block(following) if ahead else block

    def step(p, block):
        @pl.when(p == panels - 2)
        def _():
            during()

        return panel(p, block, True)

    block = lax.fori_loop(0, panels - 1, step, invert_block(work[0:PANEL, 0:PANEL]))
    if panels == 1:
        during()
    panel(panels - 1, block, False)


def padded(count, multiple):
    return (count + multiple - 1) // multiple * multiple


def dot_nt(a, b):
    return lax.dot_general(a, b, (((1,), (1,)), ((), ())), preferred_element_type=jnp.float32)


def own_pair(total_pairs):
    place = lax.axis_index("samples") * lax.axis_size("folds") + lax.axis_index("folds")
    return lax.rem(place, total_pairs), place < total_pairs


def kernel(shape, geno_hbm, trait_hbm, label_hbm, value_ref, out_ref, gram_ref, cross_ref,
           geno_ref, trait_ref, label_ref, stack, land, total, work, strip, preds_ref, slots,
           load_sem, own_sem, next_sem, next_recv, side_sem, side_recv, send_sem, recv_sem):
    chips, cores, blocks, variants, size, traits, part = shape
    z = lax.axis_index("samples")
    c = lax.axis_index("folds")
    x = lax.axis_index("blocks")
    width = stack.shape[1]
    rows_fold = width // FOLDS
    held = chips * rows_fold
    tally = chips * width - held
    own_count = FOLDS // cores
    pairs = FOLDS * SHRINK_LEVELS
    pair, reports = own_pair(pairs)
    fold, level = pair // SHRINK_LEVELS, lax.rem(pair, SHRINK_LEVELS)
    goal = fold // own_count
    local = lax.rem(fold, own_count)
    others = [lax.rem(c + o, cores) for o in range(1, cores)]
    has_left, has_right = z > 0, z < chips - 1
    last_right = ((chips - 1) * cores % pairs) // SHRINK_LEVELS
    last_left = 0
    early_right = [q for q in range(FOLDS) if q != last_right]
    early_left = [q for q in range(FOLDS) if q != last_left]

    loads = [
        pltpu.make_async_copy(source, goal_ref, load_sem.at[n])
        for n, (source, goal_ref) in enumerate(
            [(label_hbm, label_ref), (geno_hbm, geno_ref), (trait_hbm, trait_ref)]
        )
    ]
    for load in loads:
        load.start()

    barrier = pltpu.get_barrier_semaphore()

    def greet(**place):
        pl.semaphore_signal(barrier, inc=1, device_id=place, device_id_type=pl.DeviceIdType.MESH)

    for other in others:
        greet(folds=other)

    @pl.when(has_left)
    def _():
        greet(samples=z - 1)

    @pl.when(has_right)
    def _():
        greet(samples=z + 1)

    def is_self(dz, dx, dc):
        return (dz == z) & (dx == x) & (dc == c)

    senders = []
    for k in range(own_count):
        for r in range(SHRINK_LEVELS):
            place = (c * own_count + k) * SHRINK_LEVELS + r
            for b in range(blocks):
                senders.append((place // cores, b, lax.rem(place, cores), k, r))
    for sz, b, sc, k, r in senders:
        @pl.when(~is_self(sz, b, sc))
        def _():
            greet(samples=sz, blocks=b, folds=sc)

    targets = [(t, b) for t in range(chips) for b in range(blocks)]

    stack[...] = jnp.zeros_like(stack)
    total[...] = jnp.zeros_like(total)
    loads[0].wait()
    label = label_ref[...]
    fold_row = lax.broadcasted_iota(jnp.int32, (16, width), 0)
    is_fold = fold_row == label
    earlier = lax.broadcasted_iota(jnp.int32, (width, width), 0) < lax.broadcasted_iota(
        jnp.int32, (width, width), 1
    )
    rank = jnp.dot(
        is_fold.astype(jnp.bfloat16), earlier.astype(jnp.bfloat16), preferred_element_type=jnp.float32
    )
    rank = jnp.sum(jnp.where(is_fold, rank, 0.0), axis=0, keepdims=True)
    target = rank + (label * rows_fold).astype(jnp.float32)
    places = lax.broadcasted_iota(jnp.int32, (width, width), 0).astype(jnp.float32)
    permute = (places == target).astype(jnp.bfloat16)
    for load in loads[1:]:
        load.wait()
    stack[0:variants, :] = geno_ref[...]
    stack[size:size + traits, :] = trait_ref[...]
    ordered = dot_nt(stack[...], permute).astype(jnp.bfloat16)
    for q in range(FOLDS):
        for f in range(cores):
            land[z, q, f] = ordered[f * part:(f + 1) * part, q * rows_fold:(q + 1) * rows_fold]

    expected = len(others) + has_left.astype(jnp.int32) + has_right.astype(jnp.int32)
    farther = len(targets) - (goal == c).astype(jnp.int32)
    pl.semaphore_wait(barrier, expected + jnp.where(reports, farther, 0))

    def along(source, q, to, send):
        piece = land.at[source, q, c]
        return pltpu.make_async_remote_copy(
            src_ref=piece, dst_ref=piece, send_sem=send, recv_sem=next_recv.at[source, q],
            device_id={"samples": to}, device_id_type=pl.DeviceIdType.MESH,
        )

    def across(source, q, o):
        piece = land.at[source, q, c]
        return pltpu.make_async_remote_copy(
            src_ref=piece, dst_ref=piece, send_sem=side_sem.at[source, q, o],
            recv_sem=side_recv.at[source, q, o],
            device_id={"folds": others[o]}, device_id_type=pl.DeviceIdType.MESH,
        )

    def own_chunk(q, to_right):
        n, to = (0, z + 1) if to_right else (1, z - 1)
        return along(z, q, to, own_sem.at[n, q])

    for q_right, q_left in zip(early_right, early_left):
        @pl.when(has_right)
        def _():
            own_chunk(q_right, True).start()

        @pl.when(has_left)
        def _():
            own_chunk(q_left, False).start()

    def add(source, chunks):
        columns = []
        for q in chunks:
            piece = jnp.concatenate([land[source, q, f] for f in range(cores)], axis=0)
            columns.append(jnp.where(fold == q, jnp.zeros_like(piece), piece))
        both = jnp.concatenate(columns, axis=1)
        total[...] += dot_nt(both, both[0:size, :])

    add(z, range(FOLDS))

    def each_side(distance, fn):
        @pl.when(z - distance >= 0)
        def _():
            fn(z - distance, z + 1, has_right, early_right, last_right)

        @pl.when(z + distance < chips)
        def _():
            fn(z + distance, z - 1, has_left, early_left, last_left)

    def pass_on(source, q, onward, more):
        along(source, q, z, next_sem.at[source, q]).wait_recv()

        @pl.when(more)
        def _():
            along(source, q, onward, next_sem.at[source, q]).start()

        for o in range(cores - 1):
            across(source, q, o).start()

    def collect(source, onward, more, early, last):
        for q in early:
            for o in range(cores - 1):
                across(source, q, o).wait_recv()
        add(source, early)

    def receive(distance, carry):
        for n in range(FOLDS - 1):
            each_side(distance, lambda source, onward, more, early, last: pass_on(source, early[n], onward, more))

        @pl.when((z == distance) & has_right)
        def _():
            own_chunk(last_right, True).start()

        @pl.when((z + distance == chips - 1) & has_left)
        def _():
            own_chunk(last_left, False).start()

        @pl.when(distance > 1)
        def _():
            each_side(distance - 1, collect)

        return carry

    @pl.when(~has_left & has_right)
    def _():
        own_chunk(last_right, True).start()

    @pl.when(~has_right & has_left)
    def _():
        own_chunk(last_left, False).start()

    lax.fori_loop(1, chips, receive, 0)

    def idle(more, last):
        return ~more & (fold == last)

    def receive_last(distance, carry):
        def relay(source, onward, more, early, last):
            @pl.when(~idle(more, last))
            def _():
                pass_on(source, last, onward, more)

        each_side(distance, relay)
        return carry

    def collect_last(distance, carry):
        def collect_one(source, onward, more, early, last):
            @pl.when(~idle(more, last))
            def _():
                for o in range(cores - 1):
                    across(source, last, o).wait_recv()
                add(source, [last])

        each_side(distance, collect_one)
        return carry

    lax.fori_loop(1, chips, receive_last, 0)
    if chips > 1:
        each_side(chips - 1, collect)
    lax.fori_loop(1, chips, collect_last, 0)

    def late():
        def step(distance, carry):
            def relay(source, onward, more, early, last):
                @pl.when(idle(more, last))
                def _():
                    pass_on(source, last, onward, more)

            each_side(distance, relay)
            return carry

        lax.fori_loop(1, chips, step, 0)

    sub = lax.broadcasted_iota(jnp.int32, (size, size), 0)
    lane = lax.broadcasted_iota(jnp.int32, (size, size), 1)
    value = jnp.where(level == 0, value_ref[0], value_ref[SHRINK_LEVELS - 1])
    for r in range(1, SHRINK_LEVELS - 1):
        value = jnp.where(level == r, value_ref[r], value)
    added = jnp.where(sub == lane, jnp.where(sub < variants, value, 1.0), 0.0)
    total[...] = total[...] * (1.0 / tally)
    total[0:size, :] = total[0:size, :] + added
    work[...] = total[0:size, :]
    invert(work, strip, late)
    right = total[size:, :]
    inverse = split(work[...])
    first = rows_times(right, inverse)
    residual = right - rows_times(first, split(total[0:size, :]))
    betas = (first + rows_times(residual, inverse)).astype(jnp.bfloat16)

    def late_done(distance, carry):
        def wait(source, onward, more, early, last):
            @pl.when(idle(more, last))
            def _():
                for o in range(cores - 1):
                    across(source, last, o).wait_recv()

        each_side(distance, wait)
        return carry

    lax.fori_loop(1, chips, late_done, 0)
    for s in range(chips):
        chunk = jnp.concatenate([land[s, fold, f] for f in range(cores)], axis=0)
        preds = jnp.dot(betas, chunk[0:size, :], preferred_element_type=jnp.float32)
        preds_ref[:, s * rows_fold:(s + 1) * rows_fold] = preds.astype(jnp.bfloat16)

    def message(n, t, b):
        return pltpu.make_async_remote_copy(
            src_ref=preds_ref, dst_ref=slots.at[local, x, level], send_sem=send_sem.at[n],
            recv_sem=recv_sem.at[local, x, level],
            device_id={"samples": t, "blocks": b, "folds": goal}, device_id_type=pl.DeviceIdType.MESH,
        )

    @pl.when(reports)
    def _():
        for n, (t, b) in enumerate(targets):
            @pl.when(~is_self(t, b, goal))
            def _():
                message(n, t, b).start()

        @pl.when(goal == c)
        def _():
            slots[local, x, level] = preds_ref[...]

    for sz, b, sc, k, r in senders:
        @pl.when(~is_self(sz, b, sc))
        def _():
            piece = slots.at[k, b, r]
            pltpu.make_async_remote_copy(
                src_ref=piece, dst_ref=piece, send_sem=send_sem.at[0], recv_sem=recv_sem.at[k, b, r],
                device_id={"samples": sz}, device_id_type=pl.DeviceIdType.MESH,
            ).wait_recv()

    rows = slots.shape[3]

    def same_trait(mine, theirs):
        found = dot_nt(mine, theirs)
        at = lax.broadcasted_iota(jnp.int32, found.shape, 0)
        other = lax.rem(lax.broadcasted_iota(jnp.int32, found.shape, 1), rows)
        return jnp.sum(jnp.where(at == other, found, 0.0), axis=0, keepdims=True) / held

    for k in range(own_count):
        pieces = []
        for s in range(chips):
            chunk = jnp.concatenate([land[s, c * own_count + k, f] for f in range(cores)], axis=0)
            pieces.append(chunk[size:, :])
        trait = jnp.concatenate(pieces, axis=1)
        everything = jnp.concatenate(
            [slots[k, b, s] for b in range(blocks) for s in range(SHRINK_LEVELS)], axis=0
        )
        for r in range(SHRINK_LEVELS):
            mine = slots[k, x, r]
            out_ref[k, 0, r] = slots[k, x, r, 0:traits, pl.ds(pl.multiple_of(z * rows_fold, rows_fold), rows_fold)]
            found = same_trait(mine, everything)
            for b in range(blocks):
                for s in range(SHRINK_LEVELS):
                    start = (b * SHRINK_LEVELS + s) * rows
                    gram_ref[k, 0, r, b, s:s + 1, :] = found[:, start:start + traits]
            cross_ref[k, 0, r:r + 1, :] = same_trait(mine, trait)[:, 0:traits]

    @pl.when(reports)
    def _():
        for n, (t, b) in enumerate(targets):
            @pl.when(~is_self(t, b, goal))
            def _():
                message(n, t, b).wait_send()

    for q in range(FOLDS):
        @pl.when(has_right)
        def _():
            own_chunk(q, True).wait_send()

        @pl.when(has_left)
        def _():
            own_chunk(q, False).wait_send()

    def finish(distance, carry):
        def sent(source, onward, more, early, last):
            for q in range(FOLDS):
                @pl.when(more)
                def _():
                    along(source, q, onward, next_sem.at[source, q]).wait_send()

                for o in range(cores - 1):
                    across(source, q, o).wait_send()

        each_side(distance, sent)
        return carry

    lax.fori_loop(1, chips, finish, 0)


def per_device(allele_dosage_table, phenotype_values, individual_partition_label, shrink_strengths):
    chips, cores, blocks = lax.axis_size("samples"), lax.axis_size("folds"), lax.axis_size("blocks")
    variants, width = allele_dosage_table.shape
    traits = phenotype_values.shape[0]
    size = padded(variants, PANEL)
    rows = padded(size + padded(traits, 16), 16 * cores)
    part = rows // cores
    rows_fold = width // FOLDS
    held = chips * rows_fold
    own_count = FOLDS // cores
    vmem = pl.BlockSpec(memory_space=pltpu.VMEM)
    hbm = pl.BlockSpec(memory_space=pl.ANY)
    predictions, level_gram, level_cross = pl.pallas_call(
        functools.partial(kernel, (chips, cores, blocks, variants, size, traits, part)),
        out_shape=(
            jax.ShapeDtypeStruct((own_count, 1, SHRINK_LEVELS, traits, rows_fold), jnp.bfloat16),
            jax.ShapeDtypeStruct(
                (own_count, 1, SHRINK_LEVELS, blocks, SHRINK_LEVELS, traits), jnp.float32
            ),
            jax.ShapeDtypeStruct((own_count, 1, SHRINK_LEVELS, traits), jnp.float32),
        ),
        in_specs=[hbm, hbm, hbm, pl.BlockSpec(memory_space=pltpu.SMEM)],
        out_specs=(vmem,) * 3,
        scratch_shapes=[
            pltpu.VMEM((variants, width), jnp.bfloat16),
            pltpu.VMEM((traits, width), jnp.bfloat16),
            pltpu.VMEM((1, width), jnp.int32),
            pltpu.VMEM((rows, width), jnp.bfloat16),
            pltpu.VMEM((chips, FOLDS, cores, part, rows_fold), jnp.bfloat16),
            pltpu.VMEM((rows, size), jnp.float32),
            pltpu.VMEM((size, size), jnp.float32),
            pltpu.VMEM((PANEL, size), jnp.float32),
            pltpu.VMEM((rows - size, held), jnp.bfloat16),
            pltpu.VMEM((own_count, blocks, SHRINK_LEVELS, rows - size, held), jnp.bfloat16),
            pltpu.SemaphoreType.DMA((3,)),
            pltpu.SemaphoreType.DMA((2, FOLDS)),
            pltpu.SemaphoreType.DMA((chips, FOLDS)),
            pltpu.SemaphoreType.DMA((chips, FOLDS)),
            pltpu.SemaphoreType.DMA((chips, FOLDS, cores - 1)),
            pltpu.SemaphoreType.DMA((chips, FOLDS, cores - 1)),
            pltpu.SemaphoreType.DMA((chips * blocks,)),
            pltpu.SemaphoreType.DMA((own_count, blocks, SHRINK_LEVELS)),
        ],
        compiler_params=pltpu.CompilerParams(
            collective_id=0, has_side_effects=True, vmem_limit_bytes=60 * 1024 * 1024
        ),
    )(allele_dosage_table, phenotype_values, individual_partition_label.reshape(1, width), shrink_strengths)
    level_gram = jnp.transpose(level_gram, (0, 1, 2, 5, 3, 4))
    return (predictions, level_gram, level_cross)


def solution(mesh):
    in_specs = (
        P("blocks", ("groups", "samples")),
        P(None, ("groups", "samples")),
        P(("groups", "samples")),
        P(),
    )
    out_specs = (
        P("folds", "blocks", None, None, ("groups", "samples")),
        P(("groups", "folds"), "blocks", None, None, None, None),
        P(("groups", "folds"), "blocks", None, None),
    )
    return jax.shard_map(
        per_device, mesh=mesh, in_specs=in_specs, out_specs=out_specs, check_vma=False
    )
```
